128 devices in a mesh: lon: 16 (over y, x), lat: 8 (over z, core).
Axes of the slice: x: 4, y: 4, z: 4, core: 2. Of those that a mesh axis runs over, the one named last changes fastest.
Arguments:
- background_sigma: float32 [25, 192, 2048], P(None, 'lat', 'lon'), may hold values from 0.1 to 6, as said below
- scale_lon: float32 [192, 2048], P('lat', 'lon'), may hold values from 3 to 12
- scale_lat: float32 [192, 2048], P('lat', 'lon'), may hold values from 3 to 12
- obs_owner: int32 [524288], P(('lon', 'lat')), may hold values from 0 to 127, as said below
- obs_count: int32 [128], P(('lon', 'lat')), may hold values from 2048 to 4096, as said below
- obs_cell: int32 [524288], P(('lon', 'lat')), may hold values from 0 to 2942, as said below
- obs_level: int32 [524288], P(('lon', 'lat')), may hold values from 0 to 24
- obs_weight: float32 [4, 524288], P(None, ('lon', 'lat')), may hold values from 0 to 1
- obs_value: float32 [524288], P(('lon', 'lat')), may hold values from -6 to 6
- obs_precision: float32 [524288], P(('lon', 'lat')), may hold values from 5 to 50
Outputs:
- control: float32 [25, 192, 2048], P(None, 'lat', 'lon')
- increment: float32 [25, 192, 2048], P(None, 'lat', 'lon')
The draws below stay inside these ranges and needn't reach their ends.
Inputs may be any that keep to these rules, and one draw needn't show every extreme that they name: `obs_owner`: among the live slots of one device at most 64 name one owner, and in every draw some owner is named by exactly 64 live slots of every device. `obs_count`: some device has all 4096 slots live. Row obs_cell // 128 is below 23 and column obs_cell mod 128 below 127, so all four corners lie in the owner's tile. `background_sigma`: Positive.
All inputs are finite; a program needn't handle non-finite values.
Results may differ from the reference program's by a relative error of at most 0.012.
Values sent between devices are 32-bit elements; how exact they have to be, the bound alone decides.
No kernel may reach another device: no remote copies, remote signals or barrier semaphores. Data moves between devices by JAX's collectives and lax.ppermute only.
A program may use at most 64 MiB of HBM per device.

```python
import math
import jax
import jax.numpy as jnp
from jax import lax

LEV = 25
TAPS = 41
ITERS = 2
CLAT = 24
CLON = 128
OBS_DEV = 4096
NLAT = 192
NLON = 2048
NOBS = 524288
CAP = 64
N_LAT = 8
DEVICES = 128


def draw_background_sigma(key, part):
    key = jax.random.fold_in(key, 11)
    lat_frac = jnp.arange(NLAT, dtype=jnp.float32) / NLAT
    lon_frac = jnp.arange(NLON, dtype=jnp.float32) / NLON
    base_level = (0.5 + lat_frac)[:, None] * (0.6 + 1.2 * lon_frac)[None, :]
    roughness = jnp.exp(jax.random.uniform(key, (LEV, NLAT, NLON), jnp.float32, jnp.log(0.6), jnp.log(1.6)))
    return (base_level[None] * roughness).astype(jnp.float32)


def draw_obs_count(key, part):
    key = jax.random.fold_in(key, 23)
    first_key, second_key = jax.random.split(key)
    counts = OBS_DEV - jax.random.randint(first_key, (DEVICES,), 0, OBS_DEV // 2 + 1)
    fullest = jax.random.randint(second_key, (), 0, DEVICES)
    return counts.at[fullest].set(OBS_DEV).astype(jnp.int32)


def owners_of_device(key, busiest, quota):
    tickets = jnp.arange(DEVICES * CAP, dtype=jnp.int32)
    ticket_owner = tickets // CAP
    allowed = tickets % CAP < quota[ticket_owner]
    pick_key, head_key, tail_key = jax.random.split(key, 3)
    priority = jax.random.randint(pick_key, (DEVICES * CAP,), 0, 4096)
    score = jnp.where(ticket_owner == busiest, tickets, jnp.where(allowed, (priority + 1) * (DEVICES * CAP) + tickets, 2147483647))
    chosen = (jnp.argsort(score, stable=True)[:OBS_DEV] // CAP).astype(jnp.int32)
    head_count = OBS_DEV // 2
    places = jnp.concatenate([jax.random.permutation(head_key, head_count), head_count + jax.random.permutation(tail_key, OBS_DEV - head_count)])
    return jnp.zeros((OBS_DEV,), jnp.int32).at[places].set(chosen)


def draw_obs_owner(key, part):
    key = jax.random.fold_in(key, 37)
    busy_key, quota_key, device_key = jax.random.split(key, 3)
    busiest = jax.random.randint(busy_key, (), 0, DEVICES)
    halving = jax.random.randint(quota_key, (DEVICES,), 0, 2)
    quota = (CAP // jnp.left_shift(jnp.ones((DEVICES,), jnp.int32), halving)).at[busiest].set(CAP)
    device_keys = jax.random.split(device_key, DEVICES)
    owners = jax.vmap(lambda one_key: owners_of_device(one_key, busiest, quota))(device_keys)
    return owners.reshape(-1).astype(jnp.int32)


def draw_obs_cell(key, part):
    key = jax.random.fold_in(key, 53)
    row_key, column_key = jax.random.split(key)
    row_pick = jax.random.randint(row_key, (NOBS,), 0, CLAT - 1)
    column_pick = jax.random.randint(column_key, (NOBS,), 0, CLON - 1)
    return (row_pick * CLON + column_pick).astype(jnp.int32)


def set_ends(values, stream_key, least, high):
    spot = [jax.random.randint(jax.random.fold_in(stream_key, axis), (), 0, length) for axis, length in enumerate(values.shape)]
    longest = values.shape.index(max(values.shape))
    neighbour = spot[:longest] + [(spot[longest] + 1) % values.shape[longest]] + spot[longest + 1:]
    return values.at[tuple(spot)].set(least).at[tuple(neighbour)].set(high)


def shard_levels(stream_key, dims, shards, low, largest):
    def one(axis_at, parts):
        steps = jax.random.uniform(jax.random.fold_in(jax.random.fold_in(stream_key, 6), axis_at), (parts,), jnp.float32, low / len(shards), largest / len(shards))
        return jnp.repeat(jnp.exp(steps), dims[axis_at] // parts).reshape((-1,) + (1,) * (len(dims) - axis_at - 1))

    gain = one(*shards[0])
    for cut in shards[1:]:
        gain = gain * one(*cut)
    return gain


def gaussian(rng, dims, scale, reach, shards=(), held_as=jnp.bfloat16):
    gain = shard_levels(rng, dims, shards, -0.22, 0.18) if shards else 1.0
    drawn = jax.random.normal(rng, dims, jnp.float32) * scale * gain
    return jnp.minimum(jnp.maximum(drawn, -reach), reach).astype(held_as)


def setup_inputs(seed: int = 0) -> dict:
    key_list = jax.random.split(jax.random.key(seed), 11)
    return {
        "background_sigma": draw_background_sigma(jax.random.fold_in(key_list[10], 71), 0),
        "scale_lon": jnp.clip(jnp.exp(math.log(12.0) - 1.3862944 * jax.random.uniform(key_list[1], (NLAT, NLON), jnp.float32) ** shard_levels(key_list[1], (NLAT, NLON), ((0, 8), (1, 16)), -0.2, 0.2)), 3.0, 12.0),
        "scale_lat": jnp.clip(jnp.exp(math.log(12.0) - 1.3862944 * jax.random.uniform(key_list[2], (NLAT, NLON), jnp.float32) ** shard_levels(key_list[2], (NLAT, NLON), ((0, 8), (1, 16)), -0.2, 0.2)), 3.0, 12.0),
        "obs_owner": draw_obs_owner(jax.random.fold_in(key_list[10], 71), 0),
        "obs_count": draw_obs_count(jax.random.fold_in(key_list[10], 71), 0),
        "obs_cell": draw_obs_cell(jax.random.fold_in(key_list[10], 71), 0),
        "obs_level": set_ends(jax.random.randint(key_list[6], (NOBS,), 0, LEV), jax.random.fold_in(key_list[6], 1), 0, LEV - 1).astype(jnp.int32),
        "obs_weight": jnp.clip(1.0 * jax.random.uniform(key_list[7], (4, NOBS), jnp.float32) ** shard_levels(key_list[7], (4, NOBS), ((1, 128),), -0.2, 0.2), 0.0, 1.0),
        "obs_value": gaussian(key_list[8], (NOBS,), 1.0, 6.0, ((0, 128),), jnp.float32),
        "obs_precision": jnp.clip(jnp.exp(math.log(50.0) - 2.3025851 * jax.random.uniform(key_list[9], (NOBS,), jnp.float32) ** shard_levels(key_list[9], (NOBS,), ((0, 128),), -0.2, 0.2)), 5.0, 50.0),
    }


def tap_weight(tap_idx, factor, norm):
    distance = (tap_idx - TAPS // 2).astype(jnp.float32)
    return jnp.exp(-(distance * distance) * factor) / norm


def tap_norm(factor):
    def add_tap(tap_idx, total):
        distance = (tap_idx - TAPS // 2).astype(jnp.float32)
        return total + jnp.exp(-(distance * distance) * factor)
    return lax.fori_loop(0, TAPS, add_tap, jnp.zeros_like(factor))


def lon_forward(grid_field, factor, norm):
    def add_tap(tap_idx, total):
        weight = tap_weight(tap_idx, factor, norm)
        return total + weight * jnp.roll(grid_field, TAPS // 2 - tap_idx, axis=2)
    return lax.fori_loop(0, TAPS, add_tap, jnp.zeros_like(grid_field))


def lon_adjoint(gradient, factor, norm):
    def add_tap(tap_idx, total):
        weight = tap_weight(tap_idx, factor, norm)
        return total + jnp.roll(weight * gradient, tap_idx - TAPS // 2, axis=2)
    return lax.fori_loop(0, TAPS, add_tap, jnp.zeros_like(gradient))


def lat_forward(grid_field, factor, norm):
    middle = TAPS // 2
    length = grid_field.shape[1]
    padded = jnp.pad(grid_field, ((0, 0), (middle, middle), (0, 0)))

    def add_tap(tap_idx, total):
        weight = tap_weight(tap_idx, factor, norm)
        shifted = lax.dynamic_slice_in_dim(padded, tap_idx.astype(jnp.int32), length, 1)
        return total + weight * shifted
    return lax.fori_loop(0, TAPS, add_tap, jnp.zeros_like(grid_field))


def lat_adjoint(gradient, factor, norm):
    middle = TAPS // 2
    length = gradient.shape[1]
    padded = jnp.zeros((gradient.shape[0], length + 2 * middle, gradient.shape[2]), jnp.float32)

    def add_tap(tap_idx, current):
        weight = tap_weight(tap_idx, factor, norm)
        where_at = tap_idx.astype(jnp.int32)
        window = lax.dynamic_slice_in_dim(current, where_at, length, 1)
        return lax.dynamic_update_slice_in_dim(current, window + weight * gradient, where_at, 1)
    padded = lax.fori_loop(0, TAPS, add_tap, padded)
    return padded[:, middle:middle + length]


def locate(obs_owner, obs_count, obs_cell, obs_level):
    slot_index = jnp.arange(obs_owner.shape[0], dtype=jnp.int32)
    live_slot = (slot_index % OBS_DEV) < obs_count[slot_index // OBS_DEV]
    row_index = (obs_owner % N_LAT) * CLAT + obs_cell // CLON
    col_index = (obs_owner // N_LAT) * CLON + obs_cell % CLON
    base_cell = (obs_level * NLAT + row_index) * NLON + col_index
    corner = jnp.stack([base_cell, base_cell + 1, base_cell + NLON, base_cell + NLON + 1]).astype(jnp.int32)
    return live_slot, corner


def reference(background_sigma, scale_lon, scale_lat, obs_owner, obs_count, obs_cell, obs_level, obs_weight, obs_value, obs_precision):
    lon_factor = 0.5 / (scale_lon * scale_lon)
    lat_factor = 0.5 / (scale_lat * scale_lat)
    lon_norm = tap_norm(lon_factor)
    lat_norm = tap_norm(lat_factor)

    def forward(grid_field):
        return background_sigma * lat_forward(lon_forward(grid_field, lon_factor, lon_norm), lat_factor, lat_norm)

    def adjoint(gradient):
        return lon_adjoint(lat_adjoint(background_sigma * gradient, lat_factor, lat_norm), lon_factor, lon_norm)

    live_slot, corner = locate(obs_owner, obs_count, obs_cell, obs_level)
    weight_obs = obs_precision * live_slot.astype(jnp.float32)
    total_cells = background_sigma.size

    def observe(grid_field):
        return jnp.sum(obs_weight * grid_field.reshape(-1)[corner], axis=0)

    def spread(values):
        flat = jnp.zeros((total_cells,), jnp.float32).at[corner.reshape(-1)].add((obs_weight * values[None]).reshape(-1))
        return flat.reshape(background_sigma.shape)

    residual = adjoint(spread(weight_obs * obs_value))
    direction = residual
    control = jnp.zeros_like(residual)
    increment = jnp.zeros_like(residual)
    norm_now = jnp.sum(residual * residual)
    for iteration in range(ITERS):
        image_field = forward(direction)
        product = direction + adjoint(spread(weight_obs * observe(image_field)))
        step_size = norm_now / jnp.sum(direction * product)
        control = control + step_size * direction
        increment = increment + step_size * image_field
        if iteration + 1 < ITERS:
            residual = residual - step_size * product
            norm_next = jnp.sum(residual * residual)
            direction = residual + (norm_next / norm_now) * direction
            norm_now = norm_next
    return control, increment
```

```python
import functools

import jax
import jax.numpy as jnp
from jax import lax
from jax.experimental import pallas as pl
from jax.experimental.pallas import tpu as pltpu
from jax.sharding import PartitionSpec as P

TAPS = 41
HALF = TAPS // 2
LEV = 25
ROWS = 24
COLS = 128
CELLS = LEV * ROWS
HALO_COLS = 2 * HALF
SLOTS = 4096
BLOCKS = SLOTS // 128
OWNERS = 128
CAP = 64
FIELDS = 6
ROWS_PAD = 608
DAMP = 0.015625

F32 = jnp.float32
BF16 = jnp.bfloat16
NT = (((1,), (1,)), ((), ()))


def params(mib):
    return pltpu.CompilerParams(vmem_limit_bytes=mib * 1024 * 1024)


def split(x):
    high = x.astype(BF16).astype(F32)
    return high, x - high


def iota(shape, dim):
    return lax.broadcasted_iota(jnp.int32, shape, dim)


def place_kernel(
    count_ref, owner_ref, cell_ref, level_ref, weight_ref, value_ref, prec_ref, send_ref, onehot, vals
):
    count = count_ref[0]
    owner_id = iota((OWNERS, 128), 0)
    slot_id = iota((CAP, 128), 0).astype(F32)
    lane = iota((1, 128), 1)
    before = jnp.where(iota((128, 256), 0) < iota((128, 256), 1), 1.0, 0.0).astype(BF16)
    vals[12 * CAP : 13 * CAP, :] = jnp.zeros((CAP, SLOTS), BF16)
    base = jnp.zeros((OWNERS, 128), F32)
    for b in range(BLOCKS):
        at = slice(b * 128, (b + 1) * 128)
        owner = jnp.where(lane + b * 128 < count, owner_ref[b : b + 1, :], -1)
        mine = jnp.where(owner == owner_id, 1.0, 0.0)
        mine_16 = mine.astype(BF16)
        onehot[:, at] = mine_16
        ahead = jnp.dot(mine_16, before, preferred_element_type=F32)
        rank = jnp.sum(mine * (ahead[:, :128] + base), axis=0, keepdims=True)
        base = base + ahead[:, 128:]
        here = rank == slot_id
        root = jnp.sqrt(prec_ref[b : b + 1, :])
        pieces = []
        for c in range(4):
            pieces.append(split(weight_ref[c : c + 1, at] * root * DAMP))
        pieces.append(split(value_ref[b : b + 1, :] * root * (1.0 / DAMP)))
        index = level_ref[b : b + 1, :] * (ROWS * COLS) + cell_ref[b : b + 1, :]
        pieces.append(((index - (index & 1023)).astype(F32), (index & 896).astype(F32)))
        for f in range(FIELDS):
            for g in range(2):
                p = g * FIELDS + f
                vals[p * CAP : (p + 1) * CAP, at] = jnp.where(here, pieces[f][g], 0.0).astype(BF16)
        vals[13 * CAP : 14 * CAP, at] = jnp.where(here, (index & 127).astype(F32), 0.0).astype(BF16)
    placed = lax.dot_general(onehot[...], vals[...], NT, preferred_element_type=F32)
    width = FIELDS * CAP
    send_ref[:, : width - 128] = placed[:, : width - 128] + placed[:, width : 2 * width - 128]
    send_ref[:, width - 128 :] = (
        placed[:, width - 128 : width] + placed[:, 2 * width - 128 : 2 * width] + placed[:, 2 * width :]
    )


def place(obs_owner, obs_count, obs_cell, obs_level, obs_weight, obs_value, obs_precision):
    tiled = lambda x: x.reshape(BLOCKS, 128)
    vmem = pl.BlockSpec(memory_space=pltpu.VMEM)
    return pl.pallas_call(
        place_kernel,
        out_shape=jax.ShapeDtypeStruct((OWNERS, FIELDS * CAP), F32),
        in_specs=[pl.BlockSpec(memory_space=pltpu.SMEM)] + [vmem] * 6,
        out_specs=vmem,
        scratch_shapes=[pltpu.VMEM((OWNERS, SLOTS), BF16), pltpu.VMEM((14 * CAP, SLOTS), BF16)],
        compiler_params=params(24),
        name="place_observations",
    )(
        obs_count,
        tiled(obs_owner),
        tiled(obs_cell),
        tiled(obs_level),
        obs_weight,
        tiled(obs_value),
        tiled(obs_precision),
    )


RHS = (((0, 4, 0), (1, 4, 1)), ((2, 4, 0), (3, 4, 1)))
DIAG = (((0, 0, 0), (1, 1, 1)), ((2, 2, 0), (3, 3, 1)))
EAST = (((0, 1, 0),), ((2, 3, 0),))
NORTH = (((0, 2, 0), (1, 3, 1)), ((0, 3, 0),), ((1, 2, 0),))
CHUNK = 8


def accumulate(turned, blocks, onehot, highs, lows, sums):
    row_id = iota((ROWS_PAD, 128), 0)
    col_id = iota((128, 128), 0)
    for total in sums:
        total[...] = jnp.zeros_like(total)

    def step(chunk, carry):
        for kk in range(CHUNK):
            k = chunk * CHUNK + kk
            at = slice(kk * 128, (kk + 1) * 128)
            field = lambda f: turned[pl.ds(f * CAP + k, 1), :]
            index = field(5).astype(jnp.int32)
            onehot[:, at] = jnp.where((index >> 7) == row_id, 1.0, 0.0).astype(BF16)
            column = index & 127
            here = (column == col_id, column + 1 == col_id)
            for n, terms in enumerate(blocks):
                high, low = 0.0, 0.0
                for x, y, shift in terms:
                    product_high, product_low = split(field(x) * field(y))
                    high = jnp.where(here[shift], product_high, high)
                    low = jnp.where(here[shift], product_low, low)
                highs[n * 128 : (n + 1) * 128, at] = high.astype(BF16)
                lows[n * 128 : (n + 1) * 128, at] = low.astype(BF16)
        part = lax.dot_general(onehot[...], highs[...], NT, preferred_element_type=F32)
        part = part + lax.dot_general(onehot[...], lows[...], NT, preferred_element_type=F32)
        for n, total in enumerate(sums):
            total[...] += part[:, n * 128 : (n + 1) * 128]
        return carry

    lax.fori_loop(0, CAP // CHUNK, step, 0)


def row_of(ref, j):
    return ref[pl.ds(j, LEV, stride=ROWS), :]


def two_rows(sums, j):
    value = row_of(sums[0], j)
    if j > 0:
        value = value + row_of(sums[1], j - 1)
    return value


def store_sides(j, value, mid_ref, top_ref, low_ref):
    mid_ref[j] = value
    if j < HALF:
        top_ref[j] = value
    if j >= ROWS - HALF:
        low_ref[j - (ROWS - HALF)] = value


def scatter_rhs_kernel(
    got_ref, sigma_ref, mid_ref, top_ref, low_ref, turned_ref, sigma_rows_ref, onehot, highs, lows, *sums
):
    turned_ref[...] = got_ref[...].T
    accumulate(turned_ref, RHS, onehot, highs, lows, sums)
    for j in range(ROWS):
        sigma = row_of(sigma_ref, j)
        sigma_rows_ref[j] = sigma
        store_sides(j, sigma * two_rows(sums, j), mid_ref, top_ref, low_ref)


def scatter_pair_kernel(blocks, turned_ref, out_ref, onehot, highs, lows, *sums):
    accumulate(turned_ref, blocks, onehot, highs, lows, sums)
    for j in range(ROWS):
        out_ref[j] = two_rows(sums, j)


def scatter_plain_kernel(blocks, turned_ref, *refs):
    outs, (onehot, highs, lows), sums = refs[: len(blocks)], refs[len(blocks) : len(blocks) + 3], refs[len(blocks) + 3 :]
    accumulate(turned_ref, blocks, onehot, highs, lows, sums)
    for j in range(ROWS):
        for out_ref, total in zip(outs, sums):
            out_ref[j] = row_of(total, j)


def field_shape(rows=ROWS):
    return jax.ShapeDtypeStruct((rows, LEV, COLS), F32)


def scatter_scratch(count):
    return [
        pltpu.VMEM((ROWS_PAD, CHUNK * 128), BF16),
        pltpu.VMEM((count * 128, CHUNK * 128), BF16),
        pltpu.VMEM((count * 128, CHUNK * 128), BF16),
    ] + [pltpu.VMEM((ROWS_PAD, 128), F32)] * count


def scatter_cost(count):
    return pl.CostEstimate(
        flops=4 * ROWS_PAD * OWNERS * CAP * 128 * count, bytes_accessed=2 * 1024 * 1024, transcendentals=0
    )


def scatter_rhs(got, sigma):
    return pl.pallas_call(
        scatter_rhs_kernel,
        out_shape=[
            field_shape(),
            field_shape(HALF),
            field_shape(HALF),
            jax.ShapeDtypeStruct((FIELDS * CAP, OWNERS), F32),
            field_shape(),
        ],
        scratch_shapes=scatter_scratch(2),
        compiler_params=params(16),
        cost_estimate=scatter_cost(2),
        name="scatter_rhs",
    )(got, sigma)


def scatter_pair(turned, blocks, name):
    return pl.pallas_call(
        functools.partial(scatter_pair_kernel, blocks),
        out_shape=field_shape(),
        scratch_shapes=scatter_scratch(2),
        compiler_params=params(16),
        cost_estimate=scatter_cost(2),
        name=name,
    )(turned)


def scatter_plain(turned, blocks, name):
    return pl.pallas_call(
        functools.partial(scatter_plain_kernel, blocks),
        out_shape=[field_shape()] * len(blocks),
        scratch_shapes=scatter_scratch(len(blocks)),
        compiler_params=params(16),
        cost_estimate=scatter_cost(len(blocks)),
        name=name,
    )(turned)


def lon_weights_kernel(factor_ref, inverse_ref, high_ref, low_ref):
    j = pl.program_id(0)
    factor = factor_ref[pl.ds(j, 1), :]
    inverse = inverse_ref[pl.ds(j, 1), :]
    offset = ((iota((256, 256), 0) - iota((256, 256), 1) + 128) & 255) - 128
    near = jnp.abs(offset) <= HALF
    square = (offset * offset).astype(F32)
    turned = jnp.where(near, jnp.exp(-square * factor) * inverse, 0.0)
    plain = turned.T
    turned_high, turned_low = split(turned[:, :COLS])
    plain_high, plain_low = split(plain)
    turned_high, turned_low = turned_high.astype(BF16), turned_low.astype(BF16)
    plain_high, plain_low = plain_high.astype(BF16), plain_low.astype(BF16)
    gram = jnp.dot(plain_high, turned_high, preferred_element_type=F32)
    gram += jnp.dot(plain_low, turned_high, preferred_element_type=F32)
    gram += jnp.dot(plain_high, turned_low, preferred_element_type=F32)
    for n, half in enumerate((plain[:, :COLS], gram)):
        high, low = split(half)
        high_ref[0, :, n * 128 : (n + 1) * 128] = high.astype(BF16)
        low_ref[0, :, n * 128 : (n + 1) * 128] = low.astype(BF16)


def lon_weights(scale_lon):
    count = lax.axis_size("lon")
    east = [(i, (i + 1) % count) for i in range(count)]
    west = [(target, source) for source, target in east]
    from_west = lax.ppermute(scale_lon, "lon", east)
    from_east = lax.ppermute(scale_lon, "lon", west)
    lane = jnp.arange(COLS, dtype=jnp.int32)[None, :]
    valid = jnp.logical_or(lane < HALO_COLS, lane >= COLS - HALO_COLS)
    beside = jnp.where(lane < HALO_COLS, from_east, jnp.where(valid, from_west, 1.0))
    scale = jnp.concatenate([scale_lon, beside], axis=1)
    factor = 0.5 / (scale * scale)
    norm = jnp.ones_like(factor)
    for d in range(1, HALF + 1):
        norm = norm + 2.0 * jnp.exp(-float(d * d) * factor)
    used = jnp.concatenate([jnp.ones_like(valid), valid], axis=1)
    inverse = jnp.where(used, 1.0 / norm, 0.0)
    whole = pl.BlockSpec((ROWS, 256), lambda j: (0, 0))
    block = pl.BlockSpec((1, 256, 256), lambda j: (j, 0, 0))
    return pl.pallas_call(
        lon_weights_kernel,
        grid=(ROWS,),
        out_shape=[jax.ShapeDtypeStruct((ROWS, 256, 256), BF16)] * 2,
        in_specs=[whole, whole],
        out_specs=[block, block],
        compiler_params=params(16),
        name="lon_weights",
    )(factor, inverse)


def lon_kernel(q_ref, west_ref, east_ref, high_ref, low_ref, back_ref, mid_ref, top_ref, bot_ref, norm_ref, wide, both):
    lane = iota((LEV, COLS), 1)
    wide[...] = jnp.zeros_like(wide)
    norm = jnp.zeros((LEV, COLS), F32)
    for j in range(ROWS):
        group, place_in = j // 3, j % 3
        west = pltpu.roll(west_ref[group], (COLS - HALO_COLS - HALO_COLS * place_in) % COLS, 1)
        east = pltpu.roll(east_ref[group], (-HALO_COLS * place_in) % COLS, 1)
        beside = jnp.where(lane < HALO_COLS, east, jnp.where(lane >= COLS - HALO_COLS, west, 0.0))
        wide[j % 4, :LEV, :COLS] = q_ref[j]
        wide[j % 4, :LEV, COLS:] = beside
        high, low = split(wide[j % 4])
        both[j % 4, :32, :] = high.astype(BF16)
        both[j % 4, 32:, :] = low.astype(BF16)
        twice = jnp.dot(both[j % 4], high_ref[j], preferred_element_type=F32)
        more = jnp.dot(both[j % 4, :32, :], low_ref[j], preferred_element_type=F32)
        out = twice[:32] + twice[32:] + more
        back = out[:LEV, :COLS]
        back_ref[j] = back
        norm = norm + back * back
        store_sides(j, out[:LEV, COLS:], mid_ref, top_ref, bot_ref)
    norm_ref[...] = norm


def lon_both(q, from_west, from_east, weights):
    return pl.pallas_call(
        lon_kernel,
        out_shape=[
            field_shape(),
            field_shape(),
            field_shape(HALF),
            field_shape(HALF),
            jax.ShapeDtypeStruct((LEV, COLS), F32),
        ],
        scratch_shapes=[pltpu.VMEM((4, 32, 256), F32), pltpu.VMEM((4, 64, 256), BF16)],
        compiler_params=params(24),
        name="lon_transpose_and_lon",
    )(q, from_west, from_east, *weights)


def join(scratch, north_ref, mid_ref, south_ref):
    scratch[:HALF] = north_ref[...]
    scratch[HALF : HALF + ROWS] = mid_ref[...]
    scratch[HALF + ROWS :] = south_ref[...]


def lat_transpose_kernel(before_ref, mid_ref, after_ref, weight_ref, q_ref, west_ref, east_ref, wide):
    join(wide, before_ref, mid_ref, after_ref)

    def step(m, carry):
        total = jnp.zeros((LEV, COLS), F32)
        for t in range(-HALF, HALF + 1):
            at = m + (HALF + t)
            total = total + weight_ref[abs(t), pl.ds(at, 1), :] * wide[at]
        q_ref[m] = total
        return carry

    lax.fori_loop(0, ROWS, step, 0)
    lane = iota((LEV, COLS), 1)
    for group in range(ROWS // 3):
        west, east = 0.0, 0.0
        for n in range(3):
            value = q_ref[3 * group + n]
            here = jnp.logical_and(lane >= n * HALO_COLS, lane < (n + 1) * HALO_COLS)
            west = jnp.where(here, pltpu.roll(value, n * HALO_COLS, 1), west)
            east = jnp.where(here, pltpu.roll(value, (n + 1) * HALO_COLS, 1), east)
        west_ref[group] = west
        east_ref[group] = east


def lat_transpose(before, mid, after, lat_weight):
    pack = field_shape(ROWS // 3)
    return pl.pallas_call(
        lat_transpose_kernel,
        out_shape=[field_shape(), pack, pack],
        scratch_shapes=[pltpu.VMEM((ROWS + 2 * HALF, LEV, COLS), F32)],
        compiler_params=params(16),
        name="lat_transpose",
    )(before, mid, after, lat_weight)


def lat_rows(wide, weight_ref, sigma_ref, image_ref):
    def step(m, carry):
        total = weight_ref[0, pl.ds(m + HALF, 1), :] * wide[m + HALF]
        for d in range(1, HALF + 1):
            total = total + weight_ref[d, pl.ds(m + HALF, 1), :] * (wide[m + HALF - d] + wide[m + HALF + d])
        image_ref[m] = sigma_ref[m] * total
        return carry

    lax.fori_loop(0, ROWS, step, 0)


def stencil(m, x_ref, diag_ref, east_ref, north_ref, north_east_ref, north_west_ref):
    x = x_ref[m]
    right = lambda value: pltpu.roll(value, COLS - 1, 1)
    out = diag_ref[m] * x + east_ref[m] * right(x)
    moved = east_ref[m] * x
    if m + 1 < ROWS:
        above = x_ref[m + 1]
        out = out + north_ref[m] * above + north_east_ref[m] * right(above)
        moved = moved + north_west_ref[m] * above
    if m > 0:
        below = x_ref[m - 1]
        out = out + north_ref[m - 1] * below + north_west_ref[m - 1] * right(below)
        moved = moved + north_east_ref[m - 1] * below
    return x, out + pltpu.roll(moved, 1, 1)


def observe_kernel(
    before_ref, mid_ref, after_ref, weight_ref, sigma_ref, *refs
):
    coefficients, (image_ref, gmid_ref, gtop_ref, glow_ref, norm_ref, wide) = refs[:5], refs[5:]
    join(wide, before_ref, mid_ref, after_ref)
    lat_rows(wide, weight_ref, sigma_ref, image_ref)
    norm = jnp.zeros((LEV, COLS), F32)
    for m in range(ROWS):
        x, out = stencil(m, image_ref, *coefficients)
        norm = norm + x * out
        store_sides(m, sigma_ref[m] * out, gmid_ref, gtop_ref, glow_ref)
    norm_ref[...] = norm


def observe(before, mid, after, lat_weight, sigma, coefficients):
    return pl.pallas_call(
        observe_kernel,
        out_shape=[
            field_shape(),
            field_shape(),
            field_shape(HALF),
            field_shape(HALF),
            jax.ShapeDtypeStruct((LEV, COLS), F32),
        ],
        scratch_shapes=[pltpu.VMEM((ROWS + 2 * HALF, LEV, COLS), F32)],
        compiler_params=params(16),
        name="lat_and_observe",
    )(before, mid, after, lat_weight, sigma, *coefficients)


def last_kernel(before_ref, mid_ref, after_ref, weight_ref, sigma_ref, *refs):
    coefficients, norm_refs, (image_ref, sums_ref, wide) = refs[:5], refs[5:8], refs[8:]
    join(wide, before_ref, mid_ref, after_ref)
    lat_rows(wide, weight_ref, sigma_ref, image_ref)
    norm = jnp.zeros((LEV, COLS), F32)
    for m in range(ROWS):
        x, out = stencil(m, image_ref, *coefficients)
        norm = norm + x * out
    lane = iota((1, 128), 1)
    row = jnp.zeros((1, 128), F32)
    for n, value in enumerate([ref[...] for ref in norm_refs] + [norm]):
        total = jnp.sum(jnp.sum(value, axis=0, keepdims=True), axis=1, keepdims=True)
        row = jnp.where(lane == n, total, row)
    sums_ref[...] = jnp.broadcast_to(row, (OWNERS, 128))


def last(before, mid, after, lat_weight, sigma, coefficients, norms):
    return pl.pallas_call(
        last_kernel,
        out_shape=[field_shape(), jax.ShapeDtypeStruct((OWNERS, 128), F32)],
        scratch_shapes=[pltpu.VMEM((ROWS + 2 * HALF, LEV, COLS), F32)],
        compiler_params=params(16),
        name="lat_and_moments",
    )(before, mid, after, lat_weight, sigma, *coefficients, *norms)


def lat_exchange(top, low):
    count = lax.axis_size("lat")
    up = [(i, i + 1) for i in range(count - 1)]
    down = [(target, source) for source, target in up]
    return lax.ppermute(low, "lat", up), lax.ppermute(top, "lat", down)


def lon_exchange(west, east):
    count = lax.axis_size("lon")
    right = [(i, (i + 1) % count) for i in range(count)]
    left = [(target, source) for source, target in right]
    return lax.ppermute(east, "lon", right), lax.ppermute(west, "lon", left)


def lat_weights(scale_lat):
    before, after = lat_exchange(scale_lat[:HALF], scale_lat[ROWS - HALF :])
    scale = jnp.concatenate([before, scale_lat, after], axis=0)
    scale = jnp.where(scale > 0.0, scale, 1.0)
    factor = 0.5 / (scale * scale)
    square = (jnp.arange(HALF + 1, dtype=F32) ** 2)[:, None, None]
    raw = jnp.exp(-square * factor[None])
    norm = raw[0] + 2.0 * jnp.sum(raw[1:], axis=0)
    return raw / norm[None]


def combine_kernel(sums_ref, start_ref, start_image_ref, next_ref, next_image_ref, control_ref, increment_ref):
    row = jnp.sum(sums_ref[...], axis=0, keepdims=True)
    lane = iota((1, 128), 1)
    pick = lambda n: jnp.sum(jnp.where(lane == n, row, 0.0), axis=1, keepdims=True)
    m0 = pick(0)
    m1, m2, m3 = pick(1) / m0, pick(2) / m0, pick(3) / m0
    lift = 1.0 / (DAMP * DAMP)
    unit = 1.0 / lift
    step0 = unit / (unit + m1)
    keep = m1 / (unit + m1)
    ratio = jnp.maximum(m2 - m1 * m1, 0.0) / ((unit + m1) * (unit + m1))
    lead = keep + ratio
    tail = 1.0 / (unit + m1)
    second = lift * (lead * lead * m1 - 2.0 * lead * tail * m2 + tail * tail * m3)
    step1 = ratio / (ratio + ratio * ratio + second)
    alpha = step0 + step1 * lead
    gamma = -step1 * tail
    for j in range(ROWS):
        at = pl.ds(j, LEV, stride=ROWS)
        control_ref[at, :] = alpha * start_ref[j] + gamma * next_ref[j]
        increment_ref[at, :] = alpha * start_image_ref[j] + gamma * next_image_ref[j]


def combine(sums, start, start_image, following, following_image):
    return pl.pallas_call(
        combine_kernel,
        out_shape=[jax.ShapeDtypeStruct((CELLS, COLS), F32)] * 2,
        compiler_params=params(16),
        name="combine",
    )(sums, start, start_image, following, following_image)


def body(
    background_sigma,
    scale_lon,
    scale_lat,
    obs_owner,
    obs_count,
    obs_cell,
    obs_level,
    obs_weight,
    obs_value,
    obs_precision,
):
    everyone = ("lon", "lat")
    send = place(obs_owner, obs_count, obs_cell, obs_level, obs_weight, obs_value, obs_precision)
    lat_weight = lat_weights(scale_lat)
    lon_weight = lon_weights(scale_lon)
    got = lax.all_to_all(send, everyone, 0, 0, tiled=True)
    g_mid, g_top, g_low, turned, sigma = scatter_rhs(got, background_sigma.reshape(CELLS, COLS))

    before, after = lat_exchange(g_top, g_low)
    diag = scatter_pair(turned, DIAG, "scatter_diag")
    q, q_west, q_east = lat_transpose(before, g_mid, after, lat_weight)
    west, east = lon_exchange(q_west, q_east)
    side = scatter_pair(turned, EAST, "scatter_east")
    start, e_mid, e_top, e_low, norm0 = lon_both(q, west, east, lon_weight)
    before, after = lat_exchange(e_top, e_low)
    north = scatter_plain(turned, NORTH, "scatter_north")
    coefficients = (diag, side, *north)
    image0, g_mid, g_top, g_low, norm1 = observe(before, e_mid, after, lat_weight, sigma, coefficients)

    before, after = lat_exchange(g_top, g_low)
    q, q_west, q_east = lat_transpose(before, g_mid, after, lat_weight)
    west, east = lon_exchange(q_west, q_east)
    following, e_mid, e_top, e_low, norm2 = lon_both(q, west, east, lon_weight)
    before, after = lat_exchange(e_top, e_low)
    image1, sums = last(before, e_mid, after, lat_weight, sigma, coefficients, (norm0, norm1, norm2))
    sums = lax.all_to_all(sums, everyone, 0, 0, tiled=True)
    control, increment = combine(sums, start, image0, following, image1)
    shape = background_sigma.shape
    return control.reshape(shape), increment.reshape(shape)


def solution(mesh):
    return jax.shard_map(
        body,
        mesh=mesh,
        in_specs=(
            P(None, "lat", "lon"),
            P("lat", "lon"),
            P("lat", "lon"),
            P(("lon", "lat")),
            P(("lon", "lat")),
            P(("lon", "lat")),
            P(("lon", "lat")),
            P(None, ("lon", "lat")),
            P(("lon", "lat")),
            P(("lon", "lat")),
        ),
        out_specs=(P(None, "lat", "lon"), P(None, "lat", "lon")),
        check_vma=False,
    )
```

```python
import functools

import jax
import jax.numpy as jnp
from jax import lax
from jax.experimental import pallas as pl
from jax.experimental.pallas import tpu as pltpu
from jax.sharding import PartitionSpec as P

TAPS = 41
HALF = TAPS // 2
LEV = 25
ROWS = 24
COLS = 128
CELLS = LEV * ROWS
HALO_COLS = 2 * HALF
SLOTS = 4096
BLOCKS = SLOTS // 128
OWNERS = 128
CAP = 64
FIELDS = 6
BASE_ROWS = ROWS - 1
ROWS_PAD = 576
DAMP = 0.015625

F32 = jnp.float32
BF16 = jnp.bfloat16
F8 = jnp.float8_e4m3fn
NT = (((1,), (1,)), ((), ()))


def params(mib):
    return pltpu.CompilerParams(vmem_limit_bytes=mib * 1024 * 1024)


def split(x):
    high = x.astype(BF16).astype(F32)
    return high, x - high


def iota(shape, dim):
    return lax.broadcasted_iota(jnp.int32, shape, dim)


HALVES = 4


def place_kernel(fields_ref, weight_ref, send_ref, onehot, vals):
    owner_id = iota((OWNERS, 128), 0).astype(F32)
    slot_id = iota((CAP, 128), 0).astype(F32)
    before = jnp.where(iota((128, 256), 0) < iota((128, 256), 1), 1.0, 0.0).astype(BF16)
    width = FIELDS * CAP
    part = SLOTS // HALVES
    vals[12 * CAP : 13 * CAP, :] = jnp.zeros((CAP, part), BF16)
    base = jnp.zeros((OWNERS, 128), F32)
    placed = jnp.zeros((OWNERS, 14 * CAP), F32)
    for b in range(BLOCKS):
        at = slice(b * 128, (b + 1) * 128)
        to = slice(b * 128 % part, b * 128 % part + 128)
        row = lambda f: fields_ref[f, b : b + 1, :]
        mine = jnp.where(row(0) == owner_id, 1.0, 0.0)
        mine_16 = mine.astype(BF16)
        onehot[:, to] = mine_16
        ahead = jnp.dot(mine_16, before, preferred_element_type=F32)
        rank = jnp.sum(mine * (ahead[:, :128] + base), axis=0, keepdims=True)
        base = base + ahead[:, 128:]
        here = rank == slot_id
        pieces = [split(weight_ref[c : c + 1, at] * row(3)) for c in range(4)]
        pieces.append(split(row(2)))
        index = row(1).astype(jnp.int32)
        pieces.append(((index - (index & 1023)).astype(F32), (index & 896).astype(F32)))
        for f in range(FIELDS):
            for g in range(2):
                p = g * FIELDS + f
                vals[p * CAP : (p + 1) * CAP, to] = jnp.where(here, pieces[f][g], 0.0).astype(BF16)
        vals[13 * CAP : 14 * CAP, to] = jnp.where(here, (index & 127).astype(F32), 0.0).astype(BF16)
        if (b + 1) % (BLOCKS // HALVES) == 0:
            placed = placed + lax.dot_general(onehot[...], vals[...], NT, preferred_element_type=F32)
    send_ref[:, 0, : width - 128] = placed[:, : width - 128] + placed[:, width : 2 * width - 128]
    send_ref[:, 0, width - 128 :] = (
        placed[:, width - 128 : width] + placed[:, 2 * width - 128 : 2 * width] + placed[:, 2 * width :]
    )


def place(obs_owner, obs_count, obs_cell, obs_level, obs_weight, obs_value, obs_precision):
    live = jnp.arange(SLOTS, dtype=jnp.int32) < obs_count[0]
    root = jnp.sqrt(obs_precision)
    fields = jnp.stack(
        [
            jnp.where(live, obs_owner, -1).astype(F32),
            (obs_level * (BASE_ROWS * COLS) + obs_cell).astype(F32),
            obs_value * root * (1.0 / DAMP),
            root * DAMP,
        ]
    ).reshape(4, BLOCKS, 128)
    return pl.pallas_call(
        place_kernel,
        out_shape=jax.ShapeDtypeStruct((OWNERS, 1, FIELDS * CAP), F32),
        scratch_shapes=[
            pltpu.VMEM((OWNERS, SLOTS // HALVES), BF16),
            pltpu.VMEM((14 * CAP, SLOTS // HALVES), BF16),
        ],
        compiler_params=params(9),
        name="place_observations",
    )(fields, obs_weight)


RHS = (((0, 4, 0), (1, 4, 1)), ((2, 4, 0), (3, 4, 1)))
DIAG = (((0, 0, 0), (1, 1, 1)), ((2, 2, 0), (3, 3, 1)))
EAST = (((0, 1, 0),), ((2, 3, 0),))
NORTH = (((0, 2, 0), (1, 3, 1)), ((0, 3, 0),), ((1, 2, 0),))
CHUNK = 4


def low_scale(blocks):
    return 2.0**8 if blocks is RHS else 2.0**23


def build(turned, blocks, chunk, onehot, highs, lows, onehot_8, lows_8):
    zero = jnp.zeros((16, 128), BF16)
    one = jnp.ones((16, 128), BF16)
    line = iota((16, 128), 0).astype(F32)
    line_16 = line.astype(BF16)
    lines = [(line + 16.0 * n).astype(BF16) for n in range(8)]
    packed = lambda row: jnp.broadcast_to(row, (16, 128)).astype(BF16)
    for kk in range(CHUNK):
        k = chunk * CHUNK + kk
        at = slice(kk * 128, (kk + 1) * 128)
        field = lambda f: turned[pl.ds(f * CAP + k, 1), :]
        index = field(5).astype(jnp.int32)
        row = index >> 7
        fine = jnp.where(packed((row & 15).astype(F32)) == line_16, one, zero)
        coarse = packed((row >> 4).astype(F32))
        for n in range(ROWS_PAD // 16):
            onehot[n * 16 : (n + 1) * 16, at] = jnp.where(coarse == jnp.full((16, 128), n, BF16), fine, zero)
        column = (index & 127).astype(F32)
        columns = (packed(column), packed(column + 1.0))
        values = []
        for terms in blocks:
            for x, y, shift in terms:
                high, low = split(field(x) * field(y))
                values.append((packed(high), packed(low * low_scale(blocks)), shift))
        for r in range(8):
            here = [c == lines[r] for c in columns]
            done = 0
            for n, terms in enumerate(blocks):
                high, low = zero, zero
                for _ in terms:
                    value_high, value_low, shift = values[done]
                    done += 1
                    high = jnp.where(here[shift], value_high, high)
                    low = jnp.where(here[shift], value_low, low)
                highs[n * 128 + r * 16 : n * 128 + (r + 1) * 16, at] = high
                lows[n * 128 + r * 16 : n * 128 + (r + 1) * 16, at] = low
    onehot_8[...] = onehot[...].astype(F8)
    lows_8[...] = lows[...].astype(F8)


def accumulate(turned, blocks, work, sums):
    for total in sums:
        total[...] = jnp.zeros_like(total)
    first, second = work[:5], work[5:]
    steps = CAP // CHUNK
    build(turned, blocks, 0, *first)

    def multiply(onehot, highs, lows, onehot_8, lows_8):
        part = lax.dot_general(onehot[...], highs[...], NT, preferred_element_type=F32)
        rest = lax.dot_general(onehot_8[...], lows_8[...], NT, preferred_element_type=F32)
        part = part + rest * (1.0 / low_scale(blocks))
        for n, total in enumerate(sums):
            total[...] += part[:, n * 128 : (n + 1) * 128]

    def step(pair, carry):
        build(turned, blocks, 2 * pair + 1, *second)
        multiply(*first)
        build(turned, blocks, (2 * pair + 2) & (steps - 1), *first)
        multiply(*second)
        return carry

    lax.fori_loop(0, steps // 2, step, 0)


def row_of(ref, j, rows=ROWS):
    return ref[pl.ds(j, LEV, stride=rows), :]


def base_row(total, j):
    return row_of(total, j, BASE_ROWS)


def two_rows(sums, j):
    if j == 0:
        return base_row(sums[0], 0)
    if j == BASE_ROWS:
        return base_row(sums[1], j - 1)
    return base_row(sums[0], j) + base_row(sums[1], j - 1)


def even(axis):
    return lax.rem(lax.axis_index(axis), 2) == 0


def copy_sides(source_ref, top, low, a_ref, b_ref):
    is_even = even("lat")
    at_a, at_b = jnp.where(is_even, low, top), jnp.where(is_even, top, low)
    for r in range(HALF):
        a_ref[r] = source_ref[at_a + r]
        b_ref[r] = source_ref[at_b + r]


def push_rows(g_ref, weight_ref, wide):
    group = 4
    for first in range(0, ROWS + 2 * HALF, group):
        totals = [jnp.zeros((LEV, COLS), F32) for _ in range(group)]
        for j in range(max(0, first - 2 * HALF), min(ROWS, first + group)):
            g = g_ref[j]
            for n in range(group):
                distance = abs(first + n - HALF - j)
                if distance <= HALF:
                    totals[n] = totals[n] + weight_ref[distance, j : j + 1, :] * g
        for n in range(group):
            wide[first + n] = totals[n]


def push_out(g_ref, weight_ref, wide, mid_ref, a_ref, b_ref):
    push_rows(g_ref, weight_ref, wide)
    mid_ref[...] = wide[HALF : HALF + ROWS]
    copy_sides(wide, 0, HALF + ROWS, a_ref, b_ref)


def scatter_rhs_kernel(
    got_ref, sigma_ref, lat_ref, mid_ref, a_ref, b_ref, turned_ref, sigma_rows_ref, lat_weight_ref, *refs
):
    work, sums, (g, wide) = refs[:10], refs[10:12], refs[12:]
    turned_ref[...] = got_ref[...].T
    scale = lat_ref[...]
    factor = -0.5 / (scale * scale)
    norm = jnp.ones_like(factor)
    for d in range(1, HALF + 1):
        raw = jnp.exp(float(d * d) * factor)
        lat_weight_ref[d] = raw
        norm = norm + 2.0 * raw
    inverse = 1.0 / norm
    lat_weight_ref[0] = inverse
    for d in range(1, HALF + 1):
        lat_weight_ref[d] = lat_weight_ref[d] * inverse
    accumulate(turned_ref, RHS, work, sums)
    for j in range(ROWS):
        sigma = row_of(sigma_ref, j)
        sigma_rows_ref[j] = sigma
        g[j] = sigma * two_rows(sums, j)
    push_out(g, lat_weight_ref, wide, mid_ref, a_ref, b_ref)


def scatter_pair_kernel(blocks, turned_ref, out_ref, *refs):
    work, sums = refs[:10], refs[10:]
    accumulate(turned_ref, blocks, work, sums)
    for j in range(ROWS):
        out_ref[j] = two_rows(sums, j)


def scatter_plain_kernel(blocks, turned_ref, *refs):
    count = len(blocks)
    outs, work, sums = refs[:count], refs[count : count + 10], refs[count + 10 :]
    accumulate(turned_ref, blocks, work, sums)
    for j in range(ROWS):
        for out_ref, total in zip(outs, sums):
            out_ref[j] = base_row(total, j) if j < BASE_ROWS else jnp.zeros((LEV, COLS), F32)


def field_shape(rows=ROWS):
    return jax.ShapeDtypeStruct((rows, LEV, COLS), F32)


def scatter_scratch(count):
    return [
        pltpu.VMEM((ROWS_PAD, CHUNK * 128), BF16),
        pltpu.VMEM((count * 128, CHUNK * 128), BF16),
        pltpu.VMEM((count * 128, CHUNK * 128), BF16),
        pltpu.VMEM((ROWS_PAD, CHUNK * 128), F8),
        pltpu.VMEM((count * 128, CHUNK * 128), F8),
    ] * 2 + [pltpu.VMEM((ROWS_PAD, 128), F32)] * count


def row_scratch():
    return [pltpu.VMEM((ROWS, LEV, COLS), F32), pltpu.VMEM((ROWS + 2 * HALF, LEV, COLS), F32)]


def scatter_cost(count):
    return pl.CostEstimate(
        flops=4 * ROWS_PAD * OWNERS * CAP * 128 * count, bytes_accessed=2 * 1024 * 1024, transcendentals=0
    )


def scatter_rhs(got, sigma, scale_lat):
    return pl.pallas_call(
        scatter_rhs_kernel,
        out_shape=[
            field_shape(),
            field_shape(HALF),
            field_shape(HALF),
            jax.ShapeDtypeStruct((FIELDS * CAP, OWNERS), F32),
            field_shape(),
            jax.ShapeDtypeStruct((HALF + 1, ROWS, COLS), F32),
        ],
        scratch_shapes=scatter_scratch(2) + row_scratch(),
        compiler_params=params(9),
        cost_estimate=scatter_cost(2),
        name="scatter_rhs",
    )(got, sigma, scale_lat)


def scatter_pair(turned, blocks, name):
    return pl.pallas_call(
        functools.partial(scatter_pair_kernel, blocks),
        out_shape=field_shape(),
        scratch_shapes=scatter_scratch(2),
        compiler_params=params(9),
        cost_estimate=scatter_cost(2),
        name=name,
    )(turned)


def scatter_plain(turned, blocks, name):
    return pl.pallas_call(
        functools.partial(scatter_plain_kernel, blocks),
        out_shape=[field_shape()] * len(blocks),
        scratch_shapes=scatter_scratch(len(blocks)),
        compiler_params=params(9),
        cost_estimate=scatter_cost(len(blocks)),
        name=name,
    )(turned)


NEAR_TILE = tuple(range(0, 160, 16)) + (224, 240)
NEAR_SIDE = (0, 16) + tuple(range(96, 176, 16)) + (208, 224, 240)


def weights_kernel(
    lon_ref, a_ref, b_ref, high_ref, low_ref, inverse_ref,
    square, factors, columns, plain_high, plain_low, turned_high, turned_low,
):
    offset = ((iota((256, 256), 0) - iota((256, 256), 1) + 128) & 255) - 128
    square[...] = jnp.where(jnp.abs(offset) <= HALF, (offset * offset).astype(F32), 1e30)
    for ref in (plain_high, plain_low, turned_high, turned_low):
        ref[...] = jnp.zeros_like(ref)

    is_even = even("lon")
    east, west = jnp.where(is_even, a_ref[...], b_ref[...]), jnp.where(is_even, b_ref[...], a_ref[...])
    lane = iota((ROWS, COLS), 1)
    valid = jnp.logical_or(lane < HALO_COLS, lane >= COLS - HALO_COLS)
    beside = jnp.where(lane < HALO_COLS, east, jnp.where(valid, west, 1.0))
    for n, scale in enumerate((lon_ref[...], beside)):
        factor = -0.5 / (scale * scale)
        norm = jnp.ones_like(factor)
        for d in range(1, HALF + 1):
            norm = norm + 2.0 * jnp.exp(float(d * d) * factor)
        inverse = 1.0 / norm
        if n == 1:
            inverse = jnp.where(valid, inverse, 0.0)
        inverse_ref[:, n * COLS : (n + 1) * COLS] = inverse
        factors[n, :ROWS] = factor
        factors[n, ROWS:] = jnp.zeros((COLS - ROWS, COLS), F32)
        turned = factors[n].T
        for g in range(ROWS // 8):
            columns[g, n * 128 : (n + 1) * 128] = turned if g == 0 else pltpu.roll(turned, COLS - 8 * g, 1)

    def group(g, carry):
        for jj in range(8):
            j, n = 8 * g + jj, jj % 2
            factor = factors[0, pl.ds(j, 1), :]
            for r in range(0, 256, 16):
                at = slice(r, r + 16)
                column = jnp.broadcast_to(columns[g, at, jj : jj + 1], (16, 128))
                if r in NEAR_TILE:
                    high, low = split(jnp.exp(square[at, :128] * column))
                    plain_high[n, at, :128] = high.astype(BF16)
                    plain_low[n, at, :128] = low.astype(BF16)
                    high_ref[j, at, :128] = high.astype(BF16)
                    low_ref[j, at, :128] = low.astype(BF16)
                    high, low = split(jnp.exp(square[at, :128] * factor))
                    turned_high[n, at] = high.astype(BF16)
                    turned_low[n, at] = low.astype(BF16)
                else:
                    high_ref[j, at, :128] = jnp.zeros((16, 128), BF16)
                    low_ref[j, at, :128] = jnp.zeros((16, 128), BF16)
                if r in NEAR_SIDE:
                    high, low = split(jnp.exp(square[at, 128:] * column))
                    plain_high[n, at, 128:] = high.astype(BF16)
                    plain_low[n, at, 128:] = low.astype(BF16)
            gram = jnp.dot(plain_high[n], turned_high[n], preferred_element_type=F32)
            gram += jnp.dot(plain_low[n], turned_high[n], preferred_element_type=F32)
            gram += jnp.dot(plain_high[n], turned_low[n], preferred_element_type=F32)
            high, low = split(gram)
            high_ref[j, :, 128:] = high.astype(BF16)
            low_ref[j, :, 128:] = low.astype(BF16)
        return carry

    lax.fori_loop(0, ROWS // 8, group, 0)


def filter_weights(scale_lon, side_a, side_b):
    return pl.pallas_call(
        weights_kernel,
        out_shape=[jax.ShapeDtypeStruct((ROWS, 256, 256), BF16)] * 2 + [jax.ShapeDtypeStruct((ROWS, 256), F32)],
        scratch_shapes=[
            pltpu.VMEM((256, 256), F32),
            pltpu.VMEM((2, COLS, COLS), F32),
            pltpu.VMEM((ROWS // 8, 256, COLS), F32),
            pltpu.VMEM((2, 256, 256), BF16),
            pltpu.VMEM((2, 256, 256), BF16),
            pltpu.VMEM((2, 256, 128), BF16),
            pltpu.VMEM((2, 256, 128), BF16),
        ],
        compiler_params=params(9),
        cost_estimate=pl.CostEstimate(flops=2 * 10**9, bytes_accessed=8 * 1024 * 1024, transcendentals=0),
        name="filter_weights",
    )(scale_lon, side_a, side_b)


def lon_kernel(
    q_ref, ra_ref, rb_ref, high_ref, low_ref, inverse_ref, back_ref, mid_ref, a_ref, b_ref, norm_ref, wide, both
):
    lane = iota((LEV, COLS), 1)
    is_even = even("lon")
    wide[...] = jnp.zeros_like(wide)
    norm = jnp.zeros((LEV, COLS), F32)
    for j in range(ROWS):
        group, place_in = j // 3, j % 3
        ra, rb = ra_ref[group], rb_ref[group]
        east, west = jnp.where(is_even, ra, rb), jnp.where(is_even, rb, ra)
        west = pltpu.roll(west, (COLS - HALO_COLS - HALO_COLS * place_in) % COLS, 1)
        east = pltpu.roll(east, (-HALO_COLS * place_in) % COLS, 1)
        beside = jnp.where(lane < HALO_COLS, east, jnp.where(lane >= COLS - HALO_COLS, west, 0.0))
        wide[j % 4, :LEV, :COLS] = q_ref[j]
        wide[j % 4, :LEV, COLS:] = beside
        high, low = split(wide[j % 4] * inverse_ref[j : j + 1, :])
        both[j % 4, :32, :] = high.astype(BF16)
        both[j % 4, 32:, :] = low.astype(BF16)
        twice = jnp.dot(both[j % 4], high_ref[j], preferred_element_type=F32)
        more = jnp.dot(both[j % 4, :32, :], low_ref[j], preferred_element_type=F32)
        out = twice[:32] + twice[32:] + more
        back = out[:LEV, :COLS]
        back_ref[j] = back
        norm = norm + back * back
        mid_ref[j] = out[:LEV, COLS:] * inverse_ref[j : j + 1, :COLS]
    norm_ref[...] = norm
    copy_sides(mid_ref, 0, ROWS - HALF, a_ref, b_ref)


def lon_both(q, from_a, from_b, weights):
    return pl.pallas_call(
        lon_kernel,
        out_shape=[
            field_shape(),
            field_shape(),
            field_shape(HALF),
            field_shape(HALF),
            jax.ShapeDtypeStruct((LEV, COLS), F32),
        ],
        scratch_shapes=[pltpu.VMEM((4, 32, 256), F32), pltpu.VMEM((4, 64, 256), BF16)],
        compiler_params=params(9),
        name="lon_transpose_and_lon",
    )(q, from_a, from_b, *weights)


def fold_kernel(mid_ref, ra_ref, rb_ref, q_ref, a_ref, b_ref):
    is_even = even("lat")
    at_a = jnp.where(is_even, ROWS - HALF, 0)
    at_b = jnp.where(is_even, 0, ROWS - HALF)
    q_ref[...] = mid_ref[...]
    for r in range(HALF):
        q_ref[at_a + r] += ra_ref[r]
    for r in range(HALF):
        q_ref[at_b + r] += rb_ref[r]
    lane = iota((LEV, COLS), 1)
    is_even = even("lon")
    for group in range(ROWS // 3):
        west, east = 0.0, 0.0
        for n in range(3):
            value = q_ref[3 * group + n]
            here = jnp.logical_and(lane >= n * HALO_COLS, lane < (n + 1) * HALO_COLS)
            west = jnp.where(here, pltpu.roll(value, n * HALO_COLS, 1), west)
            east = jnp.where(here, pltpu.roll(value, (n + 1) * HALO_COLS, 1), east)
        a_ref[group] = jnp.where(is_even, east, west)
        b_ref[group] = jnp.where(is_even, west, east)


def fold(mid, from_a, from_b):
    pack = field_shape(ROWS // 3)
    return pl.pallas_call(
        fold_kernel,
        out_shape=[field_shape(), pack, pack],
        compiler_params=params(6),
        name="fold_rims",
    )(mid, from_a, from_b)


def lat_rows(mid_ref, ra_ref, rb_ref, wide, weight_ref, sigma_ref, image_ref):
    is_even = even("lat")
    at_a = jnp.where(is_even, HALF + ROWS, 0)
    at_b = jnp.where(is_even, 0, HALF + ROWS)
    wide[HALF : HALF + ROWS] = mid_ref[...]
    for r in range(HALF):
        wide[at_a + r] = ra_ref[r]
        wide[at_b + r] = rb_ref[r]
    group = 4
    for first in range(0, ROWS, group):
        totals = [jnp.zeros((LEV, COLS), F32) for _ in range(group)]
        for r in range(first, first + group + 2 * HALF):
            x = wide[r]
            for n in range(group):
                distance = abs(first + n + HALF - r)
                if distance <= HALF:
                    m = first + n
                    totals[n] = totals[n] + weight_ref[distance, m : m + 1, :] * x
        for n in range(group):
            image_ref[first + n] = sigma_ref[first + n] * totals[n]


def stencil(m, x_ref, diag_ref, east_ref, north_ref, north_east_ref, north_west_ref):
    x = x_ref[m]
    right = lambda value: pltpu.roll(value, COLS - 1, 1)
    out = diag_ref[m] * x + east_ref[m] * right(x)
    moved = east_ref[m] * x
    if m + 1 < ROWS:
        above = x_ref[m + 1]
        out = out + north_ref[m] * above + north_east_ref[m] * right(above)
        moved = moved + north_west_ref[m] * above
    if m > 0:
        below = x_ref[m - 1]
        out = out + north_ref[m - 1] * below + north_west_ref[m - 1] * right(below)
        moved = moved + north_east_ref[m - 1] * below
    return x, out + pltpu.roll(moved, 1, 1)


def observe_kernel(ra_ref, rb_ref, e_ref, weight_ref, sigma_ref, *refs):
    coefficients, (image_ref, mid_ref, a_ref, b_ref, norm_ref, g, wide) = refs[:5], refs[5:]
    lat_rows(e_ref, ra_ref, rb_ref, wide, weight_ref, sigma_ref, image_ref)
    norm = jnp.zeros((LEV, COLS), F32)
    for m in range(ROWS):
        x, out = stencil(m, image_ref, *coefficients)
        norm = norm + x * out
        g[m] = sigma_ref[m] * out
    norm_ref[...] = norm
    push_out(g, weight_ref, wide, mid_ref, a_ref, b_ref)


def observe(from_a, from_b, mid, lat_weight, sigma, coefficients):
    return pl.pallas_call(
        observe_kernel,
        out_shape=[
            field_shape(),
            field_shape(),
            field_shape(HALF),
            field_shape(HALF),
            jax.ShapeDtypeStruct((LEV, COLS), F32),
        ],
        scratch_shapes=row_scratch(),
        compiler_params=params(9),
        name="lat_and_observe",
    )(from_a, from_b, mid, lat_weight, sigma, *coefficients)


def last_kernel(ra_ref, rb_ref, e_ref, weight_ref, sigma_ref, *refs):
    coefficients, norm_refs, (image_ref, sums_ref, wide) = refs[:5], refs[5:8], refs[8:]
    lat_rows(e_ref, ra_ref, rb_ref, wide, weight_ref, sigma_ref, image_ref)
    norm = jnp.zeros((LEV, COLS), F32)
    for m in range(ROWS):
        x, out = stencil(m, image_ref, *coefficients)
        norm = norm + x * out
    lane = iota((1, 128), 1)
    row = jnp.zeros((1, 128), F32)
    for n, value in enumerate([ref[...] for ref in norm_refs] + [norm]):
        total = jnp.sum(jnp.sum(value, axis=0, keepdims=True), axis=1, keepdims=True)
        row = jnp.where(lane == n, total, row)
    sums_ref[...] = jnp.broadcast_to(row, (OWNERS, 128))


def last(from_a, from_b, mid, lat_weight, sigma, coefficients, norms):
    return pl.pallas_call(
        last_kernel,
        out_shape=[field_shape(), jax.ShapeDtypeStruct((OWNERS, 128), F32)],
        scratch_shapes=row_scratch()[1:],
        compiler_params=params(9),
        name="lat_and_moments",
    )(from_a, from_b, mid, lat_weight, sigma, *coefficients, *norms)


def exchange(axis, periodic, side_a, side_b):
    count = lax.axis_size(axis)

    def swaps(first):
        pairs = []
        for i in range(first, count, 2):
            if i + 1 < count or periodic:
                pairs += [(i, (i + 1) % count), ((i + 1) % count, i)]
        return pairs

    from_b = lax.ppermute(side_b, axis, swaps(1))
    return lax.ppermute(side_a, axis, swaps(0)), from_b


def combine_kernel(sums_ref, start_ref, start_image_ref, next_ref, next_image_ref, control_ref, increment_ref):
    row = jnp.sum(sums_ref[...], axis=0, keepdims=True)
    lane = iota((1, 128), 1)
    pick = lambda n: jnp.sum(jnp.where(lane == n, row, 0.0), axis=1, keepdims=True)
    m0 = pick(0)
    m1, m2, m3 = pick(1) / m0, pick(2) / m0, pick(3) / m0
    lift = 1.0 / (DAMP * DAMP)
    unit = 1.0 / lift
    step0 = unit / (unit + m1)
    keep = m1 / (unit + m1)
    ratio = jnp.maximum(m2 - m1 * m1, 0.0) / ((unit + m1) * (unit + m1))
    lead = keep + ratio
    tail = 1.0 / (unit + m1)
    second = lift * (lead * lead * m1 - 2.0 * lead * tail * m2 + tail * tail * m3)
    step1 = ratio / (ratio + ratio * ratio + second)
    alpha = step0 + step1 * lead
    gamma = -step1 * tail
    for j in range(ROWS):
        at = pl.ds(j, LEV, stride=ROWS)
        control_ref[at, :] = alpha * start_ref[j] + gamma * next_ref[j]
        increment_ref[at, :] = alpha * start_image_ref[j] + gamma * next_image_ref[j]


def combine(sums, start, start_image, following, following_image):
    return pl.pallas_call(
        combine_kernel,
        out_shape=[jax.ShapeDtypeStruct((CELLS, COLS), F32)] * 2,
        compiler_params=params(9),
        name="combine",
    )(sums, start, start_image, following, following_image)


def body(
    background_sigma,
    scale_lon,
    scale_lat,
    obs_owner,
    obs_count,
    obs_cell,
    obs_level,
    obs_weight,
    obs_value,
    obs_precision,
):
    everyone = ("lon", "lat")
    send = place(obs_owner, obs_count, obs_cell, obs_level, obs_weight, obs_value, obs_precision)
    send, scale_lon = lax.optimization_barrier((send, scale_lon))
    got = lax.all_to_all(send, everyone, 0, 0, tiled=True).reshape(OWNERS, FIELDS * CAP)
    scale_a, scale_b = exchange("lon", True, scale_lon, scale_lon)
    mid, side_a, side_b, turned, sigma, lat_weight = scatter_rhs(
        got, background_sigma.reshape(CELLS, COLS), scale_lat
    )
    turned, scale_lon, scale_a, scale_b = lax.optimization_barrier((turned, scale_lon, scale_a, scale_b))
    lon_weight = filter_weights(scale_lon, scale_a, scale_b)

    from_a, from_b = exchange("lat", False, side_a, side_b)
    north = scatter_plain(turned, NORTH, "scatter_north")
    q, side_a, side_b = fold(mid, from_a, from_b)
    from_a, from_b = exchange("lon", True, side_a, side_b)
    side = scatter_pair(turned, EAST, "scatter_east")
    start, mid, side_a, side_b, norm0 = lon_both(q, from_a, from_b, lon_weight)
    from_a, from_b = exchange("lat", False, side_a, side_b)
    diag = scatter_pair(turned, DIAG, "scatter_diag")
    coefficients = (diag, side, *north)
    image0, mid, side_a, side_b, norm1 = observe(from_a, from_b, mid, lat_weight, sigma, coefficients)

    from_a, from_b = exchange("lat", False, side_a, side_b)
    q, side_a, side_b = fold(mid, from_a, from_b)
    from_a, from_b = exchange("lon", True, side_a, side_b)
    following, mid, side_a, side_b, norm2 = lon_both(q, from_a, from_b, lon_weight)
    from_a, from_b = exchange("lat", False, side_a, side_b)
    image1, sums = last(from_a, from_b, mid, lat_weight, sigma, coefficients, (norm0, norm1, norm2))
    sums = lax.all_to_all(sums, everyone, 0, 0, tiled=True)
    control, increment = combine(sums, start, image0, following, image1)
    shape = background_sigma.shape
    return control.reshape(shape), increment.reshape(shape)


def solution(mesh):
    return jax.shard_map(
        body,
        mesh=mesh,
        in_specs=(
            P(None, "lat", "lon"),
            P("lat", "lon"),
            P("lat", "lon"),
            P(("lon", "lat")),
            P(("lon", "lat")),
            P(("lon", "lat")),
            P(("lon", "lat")),
            P(None, ("lon", "lat")),
            P(("lon", "lat")),
            P(("lon", "lat")),
        ),
        out_specs=(P(None, "lat", "lon"), P(None, "lat", "lon")),
        check_vma=False,
    )
```

```python
import functools

import jax
import jax.numpy as jnp
from jax import lax
from jax.experimental import pallas as pl
from jax.experimental.pallas import tpu as pltpu
from jax.sharding import PartitionSpec as P

TAPS = 41
HALF = TAPS // 2
LEV = 25
ROWS = 24
COLS = 128
CELLS = LEV * ROWS
HALO_COLS = 2 * HALF
SLOTS = 4096
BLOCKS = SLOTS // 128
OWNERS = 128
CAP = 64
FIELDS = 6
BASE_ROWS = ROWS - 1
ROWS_PAD = 576
DAMP = 0.015625

F32 = jnp.float32
BF16 = jnp.bfloat16
F8 = jnp.float8_e4m3fn
NT = (((1,), (1,)), ((), ()))


def params(mib):
    return pltpu.CompilerParams(vmem_limit_bytes=mib * 1024 * 1024)


def split(x):
    high = x.astype(BF16).astype(F32)
    return high, x - high


def iota(shape, dim):
    return lax.broadcasted_iota(jnp.int32, shape, dim)


HALVES = 4


def place_kernel(fields_ref, weight_ref, send_ref, onehot, vals, roots):
    roots[...] = jnp.sqrt(fields_ref[3])
    owner_id = iota((OWNERS, 128), 0).astype(F32)
    zero = jnp.zeros((16, 128), BF16)
    slots = [(iota((16, 128), 0).astype(F32) + 16.0 * n).astype(BF16) for n in range(CAP // 16)]
    packed = lambda row: jnp.broadcast_to(row, (16, 128)).astype(BF16)
    before = jnp.where(iota((128, 256), 0) < iota((128, 256), 1), 1.0, 0.0).astype(BF16)
    width = FIELDS * CAP
    part = SLOTS // HALVES
    vals[12 * CAP : 13 * CAP, :] = jnp.zeros((CAP, part), BF16)
    base = jnp.zeros((OWNERS, 128), F32)
    placed = jnp.zeros((OWNERS, 14 * CAP), F32)
    for b in range(BLOCKS):
        at = slice(b * 128, (b + 1) * 128)
        to = slice(b * 128 % part, b * 128 % part + 128)
        row = lambda f: fields_ref[f, b : b + 1, :]
        root = roots[b : b + 1, :]
        mine = jnp.where(row(0) == owner_id, 1.0, 0.0)
        mine_16 = mine.astype(BF16)
        onehot[:, to] = mine_16
        ahead = jnp.dot(mine_16, before, preferred_element_type=F32)
        rank = jnp.sum(mine * (ahead[:, :128] + base), axis=0, keepdims=True)
        base = base + ahead[:, 128:]
        here = [packed(rank) == slot for slot in slots]
        pieces = [split(weight_ref[c : c + 1, at] * (root * DAMP)) for c in range(4)]
        pieces.append(split(row(2) * (root * (1.0 / DAMP))))
        index = row(1).astype(jnp.int32)
        pieces.append(((index - (index & 1023)).astype(F32), (index & 896).astype(F32)))
        columns = [(g * FIELDS + f, pieces[f][g]) for f in range(FIELDS) for g in range(2)]
        columns.append((2 * FIELDS + 1, (index & 127).astype(F32)))
        for p, piece in columns:
            value = packed(piece)
            for n in range(CAP // 16):
                vals[p * CAP + n * 16 : p * CAP + (n + 1) * 16, to] = jnp.where(here[n], value, zero)
        if (b + 1) % (BLOCKS // HALVES) == 0:
            placed = placed + lax.dot_general(onehot[...], vals[...], NT, preferred_element_type=F32)
    send_ref[:, 0, : width - 128] = placed[:, : width - 128] + placed[:, width : 2 * width - 128]
    send_ref[:, 0, width - 128 :] = (
        placed[:, width - 128 : width] + placed[:, 2 * width - 128 : 2 * width] + placed[:, 2 * width :]
    )


def place(obs_owner, obs_count, obs_cell, obs_level, obs_weight, obs_value, obs_precision):
    live = jnp.arange(SLOTS, dtype=jnp.int32) < obs_count[0]
    kind = jnp.arange(4, dtype=jnp.int32)[:, None]
    owner = jnp.where(live, obs_owner, -1).astype(F32)[None]
    index = (obs_level * (BASE_ROWS * COLS) + obs_cell).astype(F32)[None]
    fields = jnp.where(
        kind == 0, owner, jnp.where(kind == 1, index, jnp.where(kind == 2, obs_value[None], obs_precision[None]))
    ).reshape(4, BLOCKS, 128)
    return pl.pallas_call(
        place_kernel,
        out_shape=jax.ShapeDtypeStruct((OWNERS, 1, FIELDS * CAP), F32),
        scratch_shapes=[
            pltpu.VMEM((OWNERS, SLOTS // HALVES), BF16),
            pltpu.VMEM((14 * CAP, SLOTS // HALVES), BF16),
            pltpu.VMEM((BLOCKS, 128), F32),
        ],
        compiler_params=params(9),
        name="place_observations",
    )(fields, obs_weight)


RHS = (((0, 4, 0), (1, 4, 1)), ((2, 4, 0), (3, 4, 1)))
DIAG = (((0, 0, 0), (1, 1, 1)), ((2, 2, 0), (3, 3, 1)))
EAST = (((0, 1, 0),), ((2, 3, 0),))
NORTH = (((0, 2, 0), (1, 3, 1)), ((0, 3, 0),), ((1, 2, 0),))
CHUNK = 8


def low_scale(blocks):
    return 2.0**8 if blocks is RHS else 2.0**23


def build(turned, blocks, chunk, onehot, highs, onehot_8, lows_8):
    zero = jnp.zeros((16, 128), BF16)
    one = jnp.ones((16, 128), BF16)
    line = iota((16, 128), 0).astype(F32)
    line_16 = line.astype(BF16)
    lines = [(line + 16.0 * n).astype(BF16) for n in range(8)]
    packed = lambda row: jnp.broadcast_to(row, (16, 128)).astype(BF16)
    eight = lambda pair: jnp.concatenate(pair, axis=0).astype(F8)
    for kk in range(CHUNK):
        k = chunk * CHUNK + kk
        at = slice(kk * 128, (kk + 1) * 128)
        field = lambda f: turned[pl.ds(f * CAP + k, 1), :]
        index = field(5).astype(jnp.int32)
        row = index >> 7
        fine = jnp.where(packed((row & 15).astype(F32)) == line_16, one, zero)
        coarse = packed((row >> 4).astype(F32))
        for n in range(0, ROWS_PAD // 16, 2):
            pair = [jnp.where(coarse == jnp.full((16, 128), n + i, BF16), fine, zero) for i in range(2)]
            onehot[n * 16 : (n + 1) * 16, at] = pair[0]
            onehot[(n + 1) * 16 : (n + 2) * 16, at] = pair[1]
            onehot_8[n * 16 : (n + 2) * 16, at] = eight(pair)
        column = (index & 127).astype(F32)
        columns = (packed(column), packed(column + 1.0))
        values = []
        for terms in blocks:
            for x, y, shift in terms:
                high, low = split(field(x) * field(y))
                values.append((packed(high), packed(low * low_scale(blocks)), shift))
        for r in range(0, 8, 2):
            here = [[c == lines[r + i] for c in columns] for i in range(2)]
            done = 0
            for n, terms in enumerate(blocks):
                high, low = [zero, zero], [zero, zero]
                for _ in terms:
                    value_high, value_low, shift = values[done]
                    done += 1
                    for i in range(2):
                        high[i] = jnp.where(here[i][shift], value_high, high[i])
                        low[i] = jnp.where(here[i][shift], value_low, low[i])
                start = n * 128 + r * 16
                highs[start : start + 16, at] = high[0]
                highs[start + 16 : start + 32, at] = high[1]
                lows_8[start : start + 32, at] = eight(low)


def accumulate(turned, blocks, work, sums, begin=0, end=CAP):
    first, second = work[:4], work[4:]

    def multiply(onehot, highs, onehot_8, lows_8):
        part = lax.dot_general(onehot[...], highs[...], NT, preferred_element_type=F32)
        rest = lax.dot_general(onehot_8[...], lows_8[...], NT, preferred_element_type=F32)
        part = part + rest * (1.0 / low_scale(blocks))
        for n in range(len(blocks)):
            sums[n] += part[:, n * 128 : (n + 1) * 128]

    start, steps = begin // CHUNK, (end - begin) // CHUNK
    build(turned, blocks, start, *first)
    if steps <= 3:
        for step in range(steps):
            now, later = (first, second) if step % 2 == 0 else (second, first)
            if step + 1 < steps:
                build(turned, blocks, start + step + 1, *later)
            multiply(*now)
        return

    def step(pair, carry):
        build(turned, blocks, start + 2 * pair + 1, *second)
        multiply(*first)
        build(turned, blocks, start + ((2 * pair + 2) & (steps - 1)), *first)
        multiply(*second)
        return carry

    lax.fori_loop(0, steps // 2, step, 0)


def row_of(ref, j, rows=ROWS):
    return ref[pl.ds(j, LEV, stride=rows), :]


def base_row(sums, n, j):
    return sums[n, pl.ds(j, LEV, stride=BASE_ROWS), :]


def two_rows(sums, n, j):
    if j == 0:
        return base_row(sums, n, 0)
    if j == BASE_ROWS:
        return base_row(sums, n + 1, j - 1)
    return base_row(sums, n, j) + base_row(sums, n + 1, j - 1)


def even(axis):
    return lax.rem(lax.axis_index(axis), 2) == 0


def copy_sides(source_ref, top, low, a_ref, b_ref):
    is_even = even("lat")
    at_a, at_b = jnp.where(is_even, low, top), jnp.where(is_even, top, low)
    for r in range(HALF):
        a_ref[r * LEV : (r + 1) * LEV, :] = source_ref[at_a + r]
        b_ref[r * LEV : (r + 1) * LEV, :] = source_ref[at_b + r]


def push_rows(g_ref, weight_ref, wide):
    group = 4
    for first in range(0, ROWS + 2 * HALF, group):
        totals = [jnp.zeros((LEV, COLS), F32) for _ in range(group)]
        for j in range(max(0, first - 2 * HALF), min(ROWS, first + group)):
            g = g_ref[j]
            for n in range(group):
                distance = abs(first + n - HALF - j)
                if distance <= HALF:
                    totals[n] = totals[n] + weight_ref[distance, j : j + 1, :] * g
        for n in range(group):
            wide[first + n] = totals[n]


def push_out(g_ref, weight_ref, wide, mid_ref, a_ref, b_ref):
    push_rows(g_ref, weight_ref, wide)
    mid_ref[...] = wide[HALF : HALF + ROWS]
    copy_sides(wide, 0, HALF + ROWS, a_ref, b_ref)


def scatter_rhs_kernel(
    got_ref, local_ref, mid_ref, a_ref, b_ref, turned_ref, sigma_rows_ref, lat_weight_ref, *refs
):
    work, (sums, g, wide) = refs[:8], refs[8:]
    turned_ref[...] = got_ref[...].T
    scale = local_ref[CELLS:, :]
    factor = -0.5 / (scale * scale)
    norm = jnp.ones_like(factor)
    for d in range(1, HALF + 1):
        raw = jnp.exp(float(d * d) * factor)
        lat_weight_ref[d] = raw
        norm = norm + 2.0 * raw
    inverse = 1.0 / norm
    lat_weight_ref[0] = inverse
    for d in range(1, HALF + 1):
        lat_weight_ref[d] = lat_weight_ref[d] * inverse
    sums[...] = jnp.zeros_like(sums)
    accumulate(turned_ref, RHS, work, sums)
    for j in range(ROWS):
        sigma = row_of(local_ref, j)
        sigma_rows_ref[j] = sigma
        g[j] = sigma * two_rows(sums, 0, j)
    push_out(g, lat_weight_ref, wide, mid_ref, a_ref, b_ref)


OPERATOR = DIAG + EAST + NORTH
CUTS = (0, 16, 32, CAP)


def operator_kernel(begin, end, turned_ref, *refs):
    refs = list(refs)
    before_ref = refs.pop(0) if begin > 0 else None
    if end < CAP:
        sums, work = refs[0], refs[1:]
    else:
        outs, sums, work = refs[:5], refs[5], refs[6:]
    sums[...] = jnp.zeros_like(sums) if begin == 0 else before_ref[...]
    accumulate(turned_ref, OPERATOR, work, sums, begin, end)
    if end < CAP:
        return
    for j in range(ROWS):
        outs[0][j] = two_rows(sums, 0, j)
        outs[1][j] = two_rows(sums, 2, j)
        for n in range(3):
            outs[2 + n][j] = base_row(sums, 4 + n, j) if j < BASE_ROWS else jnp.zeros((LEV, COLS), F32)


def field_shape(rows=ROWS):
    return jax.ShapeDtypeStruct((rows, LEV, COLS), F32)


def scatter_scratch(count):
    return [
        pltpu.VMEM((ROWS_PAD, CHUNK * 128), BF16),
        pltpu.VMEM((count * 128, CHUNK * 128), BF16),
        pltpu.VMEM((ROWS_PAD, CHUNK * 128), F8),
        pltpu.VMEM((count * 128, CHUNK * 128), F8),
    ] * 2


def rim_shape():
    return jax.ShapeDtypeStruct((HALF * LEV, COLS), F32)


def sums_shape(count):
    return (count, ROWS_PAD, COLS)


def row_scratch():
    return [pltpu.VMEM((ROWS, LEV, COLS), F32), pltpu.VMEM((ROWS + 2 * HALF, LEV, COLS), F32)]


def scatter_cost(count, slots=CAP):
    return pl.CostEstimate(
        flops=4 * ROWS_PAD * OWNERS * slots * 128 * count, bytes_accessed=2 * 1024 * 1024, transcendentals=0
    )


def scatter_rhs(got, local):
    return pl.pallas_call(
        scatter_rhs_kernel,
        out_shape=[
            field_shape(),
            rim_shape(),
            rim_shape(),
            jax.ShapeDtypeStruct((FIELDS * CAP, OWNERS), F32),
            field_shape(),
            jax.ShapeDtypeStruct((HALF + 1, ROWS, COLS), F32),
        ],
        scratch_shapes=scatter_scratch(2) + [pltpu.VMEM(sums_shape(2), F32)] + row_scratch(),
        compiler_params=params(9),
        cost_estimate=scatter_cost(2),
        name="scatter_rhs",
    )(got, local)


def scatter_operator(turned, part, *before):
    begin, end = CUTS[part], CUTS[part + 1]
    count = len(OPERATOR)
    final = end == CAP
    running = jax.ShapeDtypeStruct(sums_shape(count), F32)
    return pl.pallas_call(
        functools.partial(operator_kernel, begin, end),
        out_shape=[field_shape()] * 5 if final else running,
        scratch_shapes=([pltpu.VMEM(sums_shape(count), F32)] if final else []) + scatter_scratch(count),
        compiler_params=params(18),
        cost_estimate=scatter_cost(count, end - begin),
        name="scatter_operator",
    )(turned, *before)


NEAR_TILE = tuple(range(0, 160, 16)) + (224, 240)
NEAR_SIDE = (0, 16) + tuple(range(96, 176, 16)) + (208, 224, 240)


def weights_kernel(
    lon_ref, a_ref, b_ref, high_ref, low_ref, inverse_ref,
    square, factors, columns, plain_high, plain_low, turned_high, turned_low,
):
    offset = ((iota((256, 256), 0) - iota((256, 256), 1) + 128) & 255) - 128
    square[...] = jnp.where(jnp.abs(offset) <= HALF, (offset * offset).astype(F32), 1e30)
    for ref in (plain_high, plain_low, turned_high, turned_low):
        ref[...] = jnp.zeros_like(ref)

    is_even = even("lon")
    east, west = jnp.where(is_even, a_ref[...], b_ref[...]), jnp.where(is_even, b_ref[...], a_ref[...])
    lane = iota((ROWS, COLS), 1)
    valid = jnp.logical_or(lane < HALO_COLS, lane >= COLS - HALO_COLS)
    beside = jnp.where(lane < HALO_COLS, east, jnp.where(valid, west, 1.0))
    for n, scale in enumerate((lon_ref[...], beside)):
        factor = -0.5 / (scale * scale)
        norm = jnp.ones_like(factor)
        for d in range(1, HALF + 1):
            norm = norm + 2.0 * jnp.exp(float(d * d) * factor)
        inverse = 1.0 / norm
        if n == 1:
            inverse = jnp.where(valid, inverse, 0.0)
        inverse_ref[:, n * COLS : (n + 1) * COLS] = inverse
        factors[n, :ROWS] = factor
        factors[n, ROWS:] = jnp.zeros((COLS - ROWS, COLS), F32)
        turned = factors[n].T
        for g in range(ROWS // 8):
            columns[g, n * 128 : (n + 1) * 128] = turned if g == 0 else pltpu.roll(turned, COLS - 8 * g, 1)

    def group(g, carry):
        for jj in range(8):
            j, n = 8 * g + jj, jj % 2
            factor = factors[0, pl.ds(j, 1), :]
            for r in range(0, 256, 16):
                at = slice(r, r + 16)
                column = jnp.broadcast_to(columns[g, at, jj : jj + 1], (16, 128))
                if r in NEAR_TILE:
                    high, low = split(jnp.exp(square[at, :128] * column))
                    plain_high[n, at, :128] = high.astype(BF16)
                    plain_low[n, at, :128] = low.astype(BF16)
                    high_ref[j, at, :128] = high.astype(BF16)
                    low_ref[j, at, :128] = low.astype(BF16)
                    high, low = split(jnp.exp(square[at, :128] * factor))
                    turned_high[n, at] = high.astype(BF16)
                    turned_low[n, at] = low.astype(BF16)
                else:
                    high_ref[j, at, :128] = jnp.zeros((16, 128), BF16)
                    low_ref[j, at, :128] = jnp.zeros((16, 128), BF16)
                if r in NEAR_SIDE:
                    high, low = split(jnp.exp(square[at, 128:] * column))
                    plain_high[n, at, 128:] = high.astype(BF16)
                    plain_low[n, at, 128:] = low.astype(BF16)
            gram = jnp.dot(plain_high[n], turned_high[n], preferred_element_type=F32)
            gram += jnp.dot(plain_low[n], turned_high[n], preferred_element_type=F32)
            gram += jnp.dot(plain_high[n], turned_low[n], preferred_element_type=F32)
            high, low = split(gram)
            high_ref[j, :, 128:] = high.astype(BF16)
            low_ref[j, :, 128:] = low.astype(BF16)
        return carry

    lax.fori_loop(0, ROWS // 8, group, 0)


def filter_weights(scale_lon, side_a, side_b):
    return pl.pallas_call(
        weights_kernel,
        out_shape=[jax.ShapeDtypeStruct((ROWS, 256, 256), BF16)] * 2 + [jax.ShapeDtypeStruct((ROWS, 256), F32)],
        scratch_shapes=[
            pltpu.VMEM((256, 256), F32),
            pltpu.VMEM((2, COLS, COLS), F32),
            pltpu.VMEM((ROWS // 8, 256, COLS), F32),
            pltpu.VMEM((2, 256, 256), BF16),
            pltpu.VMEM((2, 256, 256), BF16),
            pltpu.VMEM((2, 256, 128), BF16),
            pltpu.VMEM((2, 256, 128), BF16),
        ],
        compiler_params=params(9),
        cost_estimate=pl.CostEstimate(flops=2 * 10**9, bytes_accessed=8 * 1024 * 1024, transcendentals=0),
        name="filter_weights",
    )(scale_lon, side_a, side_b)


def lon_kernel(
    q_ref, ra_ref, rb_ref, high_ref, low_ref, inverse_ref, back_ref, mid_ref, a_ref, b_ref, norm_ref, wide, both
):
    lane = iota((LEV, COLS), 1)
    is_even = even("lon")
    wide[...] = jnp.zeros_like(wide)
    norm = jnp.zeros((LEV, COLS), F32)
    for j in range(ROWS):
        group, place_in = j // 3, j % 3
        ra, rb = ra_ref[group], rb_ref[group]
        east, west = jnp.where(is_even, ra, rb), jnp.where(is_even, rb, ra)
        west = pltpu.roll(west, (COLS - HALO_COLS - HALO_COLS * place_in) % COLS, 1)
        east = pltpu.roll(east, (-HALO_COLS * place_in) % COLS, 1)
        beside = jnp.where(lane < HALO_COLS, east, jnp.where(lane >= COLS - HALO_COLS, west, 0.0))
        wide[j % 4, :LEV, :COLS] = q_ref[j]
        wide[j % 4, :LEV, COLS:] = beside
        high, low = split(wide[j % 4] * inverse_ref[j : j + 1, :])
        both[j % 4, :32, :] = high.astype(BF16)
        both[j % 4, 32:, :] = low.astype(BF16)
        twice = jnp.dot(both[j % 4], high_ref[j], preferred_element_type=F32)
        more = jnp.dot(both[j % 4, :32, :], low_ref[j], preferred_element_type=F32)
        out = twice[:32] + twice[32:] + more
        back = out[:LEV, :COLS]
        back_ref[j] = back
        norm = norm + back * back
        mid_ref[j] = out[:LEV, COLS:] * inverse_ref[j : j + 1, :COLS]
    norm_ref[...] = norm
    copy_sides(mid_ref, 0, ROWS - HALF, a_ref, b_ref)


def lon_both(q, from_a, from_b, weights):
    return pl.pallas_call(
        lon_kernel,
        out_shape=[
            field_shape(),
            field_shape(),
            rim_shape(),
            rim_shape(),
            jax.ShapeDtypeStruct((LEV, COLS), F32),
        ],
        scratch_shapes=[pltpu.VMEM((4, 32, 256), F32), pltpu.VMEM((4, 64, 256), BF16)],
        compiler_params=params(9),
        name="lon_transpose_and_lon",
    )(q, from_a, from_b, *weights)


def fold_kernel(mid_ref, ra_ref, rb_ref, q_ref, a_ref, b_ref):
    is_even = even("lat")
    at_a = jnp.where(is_even, ROWS - HALF, 0)
    at_b = jnp.where(is_even, 0, ROWS - HALF)
    q_ref[...] = mid_ref[...]
    for r in range(HALF):
        q_ref[at_a + r] += ra_ref[r * LEV : (r + 1) * LEV, :]
    for r in range(HALF):
        q_ref[at_b + r] += rb_ref[r * LEV : (r + 1) * LEV, :]
    lane = iota((LEV, COLS), 1)
    is_even = even("lon")
    for group in range(ROWS // 3):
        west, east = 0.0, 0.0
        for n in range(3):
            value = q_ref[3 * group + n]
            here = jnp.logical_and(lane >= n * HALO_COLS, lane < (n + 1) * HALO_COLS)
            west = jnp.where(here, pltpu.roll(value, n * HALO_COLS, 1), west)
            east = jnp.where(here, pltpu.roll(value, (n + 1) * HALO_COLS, 1), east)
        a_ref[group] = jnp.where(is_even, east, west)
        b_ref[group] = jnp.where(is_even, west, east)


def fold(mid, from_a, from_b):
    pack = field_shape(ROWS // 3)
    return pl.pallas_call(
        fold_kernel,
        out_shape=[field_shape(), pack, pack],
        compiler_params=params(6),
        name="fold_rims",
    )(mid, from_a, from_b)


def lat_rows(mid_ref, ra_ref, rb_ref, wide, weight_ref, sigma_ref, image_ref):
    is_even = even("lat")
    at_a = jnp.where(is_even, HALF + ROWS, 0)
    at_b = jnp.where(is_even, 0, HALF + ROWS)
    wide[HALF : HALF + ROWS] = mid_ref[...]
    for r in range(HALF):
        wide[at_a + r] = ra_ref[r * LEV : (r + 1) * LEV, :]
        wide[at_b + r] = rb_ref[r * LEV : (r + 1) * LEV, :]
    group = 4
    for first in range(0, ROWS, group):
        totals = [jnp.zeros((LEV, COLS), F32) for _ in range(group)]
        for r in range(first, first + group + 2 * HALF):
            x = wide[r]
            for n in range(group):
                distance = abs(first + n + HALF - r)
                if distance <= HALF:
                    m = first + n
                    totals[n] = totals[n] + weight_ref[distance, m : m + 1, :] * x
        for n in range(group):
            image_ref[first + n] = sigma_ref[first + n] * totals[n]


def stencil(m, x_ref, diag_ref, east_ref, north_ref, north_east_ref, north_west_ref):
    x = x_ref[m]
    right = lambda value: pltpu.roll(value, COLS - 1, 1)
    out = diag_ref[m] * x + east_ref[m] * right(x)
    moved = east_ref[m] * x
    if m + 1 < ROWS:
        above = x_ref[m + 1]
        out = out + north_ref[m] * above + north_east_ref[m] * right(above)
        moved = moved + north_west_ref[m] * above
    if m > 0:
        below = x_ref[m - 1]
        out = out + north_ref[m - 1] * below + north_west_ref[m - 1] * right(below)
        moved = moved + north_east_ref[m - 1] * below
    return x, out + pltpu.roll(moved, 1, 1)


def observe_kernel(ra_ref, rb_ref, e_ref, weight_ref, sigma_ref, *refs):
    coefficients, (image_ref, mid_ref, a_ref, b_ref, norm_ref, g, wide) = refs[:5], refs[5:]
    lat_rows(e_ref, ra_ref, rb_ref, wide, weight_ref, sigma_ref, image_ref)
    norm = jnp.zeros((LEV, COLS), F32)
    for m in range(ROWS):
        x, out = stencil(m, image_ref, *coefficients)
        norm = norm + x * out
        g[m] = sigma_ref[m] * out
    norm_ref[...] = norm
    push_out(g, weight_ref, wide, mid_ref, a_ref, b_ref)


def observe(from_a, from_b, mid, lat_weight, sigma, coefficients):
    return pl.pallas_call(
        observe_kernel,
        out_shape=[
            field_shape(),
            field_shape(),
            rim_shape(),
            rim_shape(),
            jax.ShapeDtypeStruct((LEV, COLS), F32),
        ],
        scratch_shapes=row_scratch(),
        compiler_params=params(9),
        name="lat_and_observe",
    )(from_a, from_b, mid, lat_weight, sigma, *coefficients)


def last_kernel(ra_ref, rb_ref, e_ref, weight_ref, sigma_ref, *refs):
    coefficients, norm_refs, (image_ref, sums_ref, wide) = refs[:5], refs[5:8], refs[8:]
    lat_rows(e_ref, ra_ref, rb_ref, wide, weight_ref, sigma_ref, image_ref)
    norm = jnp.zeros((LEV, COLS), F32)
    for m in range(ROWS):
        x, out = stencil(m, image_ref, *coefficients)
        norm = norm + x * out
    lane = iota((1, 128), 1)
    row = jnp.zeros((1, 128), F32)
    for n, value in enumerate([ref[...] for ref in norm_refs] + [norm]):
        total = jnp.sum(jnp.sum(value, axis=0, keepdims=True), axis=1, keepdims=True)
        row = jnp.where(lane == n, total, row)
    sums_ref[...] = jnp.broadcast_to(row, (OWNERS, 128))


def last(from_a, from_b, mid, lat_weight, sigma, coefficients, norms):
    return pl.pallas_call(
        last_kernel,
        out_shape=[field_shape(), jax.ShapeDtypeStruct((OWNERS, 128), F32)],
        scratch_shapes=row_scratch()[1:],
        compiler_params=params(9),
        name="lat_and_moments",
    )(from_a, from_b, mid, lat_weight, sigma, *coefficients, *norms)


def exchange(axis, periodic, side_a, side_b):
    count = lax.axis_size(axis)

    def swaps(first):
        pairs = []
        for i in range(first, count, 2):
            if i + 1 < count or periodic:
                pairs += [(i, (i + 1) % count), ((i + 1) % count, i)]
        return pairs

    from_b = lax.ppermute(side_b, axis, swaps(1))
    return lax.ppermute(side_a, axis, swaps(0)), from_b


def combine_kernel(sums_ref, start_ref, start_image_ref, next_ref, next_image_ref, control_ref, increment_ref):
    row = jnp.sum(sums_ref[...], axis=0, keepdims=True)
    lane = iota((1, 128), 1)
    pick = lambda n: jnp.sum(jnp.where(lane == n, row, 0.0), axis=1, keepdims=True)
    m0 = pick(0)
    m1, m2, m3 = pick(1) / m0, pick(2) / m0, pick(3) / m0
    lift = 1.0 / (DAMP * DAMP)
    unit = 1.0 / lift
    step0 = unit / (unit + m1)
    keep = m1 / (unit + m1)
    ratio = jnp.maximum(m2 - m1 * m1, 0.0) / ((unit + m1) * (unit + m1))
    lead = keep + ratio
    tail = 1.0 / (unit + m1)
    second = lift * (lead * lead * m1 - 2.0 * lead * tail * m2 + tail * tail * m3)
    step1 = ratio / (ratio + ratio * ratio + second)
    alpha = step0 + step1 * lead
    gamma = -step1 * tail
    for j in range(ROWS):
        at = pl.ds(j, LEV, stride=ROWS)
        control_ref[at, :] = alpha * start_ref[j] + gamma * next_ref[j]
        increment_ref[at, :] = alpha * start_image_ref[j] + gamma * next_image_ref[j]


def combine(sums, start, start_image, following, following_image):
    return pl.pallas_call(
        combine_kernel,
        out_shape=[jax.ShapeDtypeStruct((CELLS, COLS), F32)] * 2,
        compiler_params=params(9),
        name="combine",
    )(sums, start, start_image, following, following_image)


def body(
    background_sigma,
    scale_lon,
    scale_lat,
    obs_owner,
    obs_count,
    obs_cell,
    obs_level,
    obs_weight,
    obs_value,
    obs_precision,
):
    everyone = ("lon", "lat")
    send = place(obs_owner, obs_count, obs_cell, obs_level, obs_weight, obs_value, obs_precision)
    send, scale_lon = lax.optimization_barrier((send, scale_lon))
    got = lax.all_to_all(send, everyone, 0, 0, tiled=True).reshape(OWNERS, FIELDS * CAP)
    scale_a, scale_b = exchange("lon", True, scale_lon, scale_lon)
    local = jnp.concatenate([background_sigma.reshape(CELLS, COLS), scale_lat], axis=0)
    mid, side_a, side_b, turned, sigma, lat_weight = scatter_rhs(got, local)
    turned, scale_lon, scale_a, scale_b = lax.optimization_barrier((turned, scale_lon, scale_a, scale_b))
    lon_weight = filter_weights(scale_lon, scale_a, scale_b)

    from_a, from_b = exchange("lat", False, side_a, side_b)
    sums = scatter_operator(turned, 0)
    q, side_a, side_b = fold(mid, from_a, from_b)
    from_a, from_b = exchange("lon", True, side_a, side_b)
    sums = scatter_operator(turned, 1, sums)
    start, mid, side_a, side_b, norm0 = lon_both(q, from_a, from_b, lon_weight)
    from_a, from_b = exchange("lat", False, side_a, side_b)
    coefficients = scatter_operator(turned, 2, sums)
    image0, mid, side_a, side_b, norm1 = observe(from_a, from_b, mid, lat_weight, sigma, coefficients)

    from_a, from_b = exchange("lat", False, side_a, side_b)
    q, side_a, side_b = fold(mid, from_a, from_b)
    from_a, from_b = exchange("lon", True, side_a, side_b)
    following, mid, side_a, side_b, norm2 = lon_both(q, from_a, from_b, lon_weight)
    from_a, from_b = exchange("lat", False, side_a, side_b)
    image1, sums = last(from_a, from_b, mid, lat_weight, sigma, coefficients, (norm0, norm1, norm2))
    sums = lax.all_to_all(sums, everyone, 0, 0, tiled=True)
    control, increment = combine(sums, start, image0, following, image1)
    shape = background_sigma.shape
    return control.reshape(shape), increment.reshape(shape)


def solution(mesh):
    return jax.shard_map(
        body,
        mesh=mesh,
        in_specs=(
            P(None, "lat", "lon"),
            P("lat", "lon"),
            P("lat", "lon"),
            P(("lon", "lat")),
            P(("lon", "lat")),
            P(("lon", "lat")),
            P(("lon", "lat")),
            P(None, ("lon", "lat")),
            P(("lon", "lat")),
            P(("lon", "lat")),
        ),
        out_specs=(P(None, "lat", "lon"), P(None, "lat", "lon")),
        check_vma=False,
    )
```

```python
import functools

import jax
import jax.numpy as jnp
from jax import lax
from jax.experimental import pallas as pl
from jax.experimental.pallas import tpu as pltpu
from jax.sharding import PartitionSpec as P

TAPS = 41
HALF = TAPS // 2
LEV = 25
ROWS = 24
COLS = 128
CELLS = LEV * ROWS
HALO_COLS = 2 * HALF
SLOTS = 4096
BLOCKS = SLOTS // 128
OWNERS = 128
CAP = 64
FIELDS = 6
BASE_ROWS = ROWS - 1
ROWS_PAD = 576
DAMP = 0.015625

F32 = jnp.float32
BF16 = jnp.bfloat16
F8 = jnp.float8_e4m3fn
NT = (((1,), (1,)), ((), ()))


def params(mib):
    return pltpu.CompilerParams(vmem_limit_bytes=mib * 1024 * 1024)


def split(x):
    high = x.astype(BF16).astype(F32)
    return high, x - high


def iota(shape, dim):
    return lax.broadcasted_iota(jnp.int32, shape, dim)


HALVES = 4


def place_kernel(fields_ref, weight_ref, send_ref, onehot, vals, roots):
    roots[...] = jnp.sqrt(fields_ref[3])
    owner_id = iota((OWNERS, 128), 0).astype(F32)
    zero = jnp.zeros((16, 128), BF16)
    slots = [(iota((16, 128), 0).astype(F32) + 16.0 * n).astype(BF16) for n in range(CAP // 16)]
    packed = lambda row: jnp.broadcast_to(row, (16, 128)).astype(BF16)
    before = jnp.where(iota((128, 256), 0) < iota((128, 256), 1), 1.0, 0.0).astype(BF16)
    width = FIELDS * CAP
    part = SLOTS // HALVES
    vals[12 * CAP : 13 * CAP, :] = jnp.zeros((CAP, part), BF16)
    base = jnp.zeros((OWNERS, 128), F32)
    placed = jnp.zeros((OWNERS, 14 * CAP), F32)
    for b in range(BLOCKS):
        at = slice(b * 128, (b + 1) * 128)
        to = slice(b * 128 % part, b * 128 % part + 128)
        row = lambda f: fields_ref[f, b : b + 1, :]
        root = roots[b : b + 1, :]
        mine = jnp.where(row(0) == owner_id, 1.0, 0.0)
        mine_16 = mine.astype(BF16)
        onehot[:, to] = mine_16
        ahead = jnp.dot(mine_16, before, preferred_element_type=F32)
        rank = jnp.sum(mine * (ahead[:, :128] + base), axis=0, keepdims=True)
        base = base + ahead[:, 128:]
        here = [packed(rank) == slot for slot in slots]
        pieces = [split(weight_ref[c : c + 1, at] * (root * DAMP)) for c in range(4)]
        pieces.append(split(row(2) * (root * (1.0 / DAMP))))
        index = row(1).astype(jnp.int32)
        pieces.append(((index - (index & 1023)).astype(F32), (index & 896).astype(F32)))
        columns = [(g * FIELDS + f, pieces[f][g]) for f in range(FIELDS) for g in range(2)]
        columns.append((2 * FIELDS + 1, (index & 127).astype(F32)))
        for p, piece in columns:
            value = packed(piece)
            for n in range(CAP // 16):
                vals[p * CAP + n * 16 : p * CAP + (n + 1) * 16, to] = jnp.where(here[n], value, zero)
        if (b + 1) % (BLOCKS // HALVES) == 0:
            placed = placed + lax.dot_general(onehot[...], vals[...], NT, preferred_element_type=F32)
    send_ref[:, 0, : width - 128] = placed[:, : width - 128] + placed[:, width : 2 * width - 128]
    send_ref[:, 0, width - 128 :] = (
        placed[:, width - 128 : width] + placed[:, 2 * width - 128 : 2 * width] + placed[:, 2 * width :]
    )


def place(obs_owner, obs_count, obs_cell, obs_level, obs_weight, obs_value, obs_precision):
    live = jnp.arange(SLOTS, dtype=jnp.int32) < obs_count[0]
    kind = jnp.arange(4, dtype=jnp.int32)[:, None]
    owner = jnp.where(live, obs_owner, -1).astype(F32)[None]
    index = (obs_level * (BASE_ROWS * COLS) + obs_cell).astype(F32)[None]
    fields = jnp.where(
        kind == 0, owner, jnp.where(kind == 1, index, jnp.where(kind == 2, obs_value[None], obs_precision[None]))
    ).reshape(4, BLOCKS, 128)
    return pl.pallas_call(
        place_kernel,
        out_shape=jax.ShapeDtypeStruct((OWNERS, 1, FIELDS * CAP), F32),
        scratch_shapes=[
            pltpu.VMEM((OWNERS, SLOTS // HALVES), BF16),
            pltpu.VMEM((14 * CAP, SLOTS // HALVES), BF16),
            pltpu.VMEM((BLOCKS, 128), F32),
        ],
        compiler_params=params(9),
        name="place_observations",
    )(fields, obs_weight)


RHS = (((0, 4, 0), (1, 4, 1)), ((2, 4, 0), (3, 4, 1)))
DIAG = (((0, 0, 0), (1, 1, 1)), ((2, 2, 0), (3, 3, 1)))
EAST = (((0, 1, 0),), ((2, 3, 0),))
NORTH = (((0, 2, 0), (1, 3, 1)), ((0, 3, 0),), ((1, 2, 0),))
CHUNK = 8


def low_scale(blocks):
    return 2.0**8 if blocks is RHS else 2.0**23


def build(turned, blocks, chunk, onehot, highs, onehot_8, lows_8):
    zero = jnp.zeros((16, 128), BF16)
    one = jnp.ones((16, 128), BF16)
    line = iota((16, 128), 0).astype(F32)
    line_16 = line.astype(BF16)
    lines = [(line + 16.0 * n).astype(BF16) for n in range(8)]
    packed = lambda row: jnp.broadcast_to(row, (16, 128)).astype(BF16)
    eight = lambda pair: jnp.concatenate(pair, axis=0).astype(F8)
    for kk in range(CHUNK):
        k = chunk * CHUNK + kk
        at = slice(kk * 128, (kk + 1) * 128)
        field = lambda f: turned[pl.ds(f * CAP + k, 1), :]
        index = field(5).astype(jnp.int32)
        row = index >> 7
        fine = jnp.where(packed((row & 15).astype(F32)) == line_16, one, zero)
        coarse = packed((row >> 4).astype(F32))
        for n in range(0, ROWS_PAD // 16, 2):
            pair = [jnp.where(coarse == jnp.full((16, 128), n + i, BF16), fine, zero) for i in range(2)]
            onehot[n * 16 : (n + 1) * 16, at] = pair[0]
            onehot[(n + 1) * 16 : (n + 2) * 16, at] = pair[1]
            onehot_8[n * 16 : (n + 2) * 16, at] = eight(pair)
        column = (index & 127).astype(F32)
        columns = (packed(column), packed(column + 1.0))
        values = []
        for terms in blocks:
            for x, y, shift in terms:
                high, low = split(field(x) * field(y))
                values.append((packed(high), packed(low * low_scale(blocks)), shift))
        for r in range(0, 8, 2):
            here = [[c == lines[r + i] for c in columns] for i in range(2)]
            done = 0
            for n, terms in enumerate(blocks):
                high, low = [zero, zero], [zero, zero]
                for _ in terms:
                    value_high, value_low, shift = values[done]
                    done += 1
                    for i in range(2):
                        high[i] = jnp.where(here[i][shift], value_high, high[i])
                        low[i] = jnp.where(here[i][shift], value_low, low[i])
                start = n * 128 + r * 16
                highs[start : start + 16, at] = high[0]
                highs[start + 16 : start + 32, at] = high[1]
                lows_8[start : start + 32, at] = eight(low)


def accumulate(turned, blocks, work, sums, begin=0, end=CAP):
    first, second = work[:4], work[4:]

    def multiply(onehot, highs, onehot_8, lows_8):
        part = lax.dot_general(onehot[...], highs[...], NT, preferred_element_type=F32)
        rest = lax.dot_general(onehot_8[...], lows_8[...], NT, preferred_element_type=F32)
        part = part + rest * (1.0 / low_scale(blocks))
        for n in range(len(blocks)):
            sums[n] += part[:, n * 128 : (n + 1) * 128]

    start, steps = begin // CHUNK, (end - begin) // CHUNK
    build(turned, blocks, start, *first)
    if steps <= 3:
        for step in range(steps):
            now, later = (first, second) if step % 2 == 0 else (second, first)
            if step + 1 < steps:
                build(turned, blocks, start + step + 1, *later)
            multiply(*now)
        return

    def step(pair, carry):
        build(turned, blocks, start + 2 * pair + 1, *second)
        multiply(*first)
        build(turned, blocks, start + ((2 * pair + 2) & (steps - 1)), *first)
        multiply(*second)
        return carry

    lax.fori_loop(0, steps // 2, step, 0)


def row_of(ref, j, rows=ROWS):
    return ref[pl.ds(j, LEV, stride=rows), :]


def base_row(sums, n, j):
    return sums[n, pl.ds(j, LEV, stride=BASE_ROWS), :]


def two_rows(sums, n, j):
    if j == 0:
        return base_row(sums, n, 0)
    if j == BASE_ROWS:
        return base_row(sums, n + 1, j - 1)
    return base_row(sums, n, j) + base_row(sums, n + 1, j - 1)


def even(axis):
    return lax.rem(lax.axis_index(axis), 2) == 0


def copy_sides(source_ref, top, low, a_ref, b_ref):
    is_even = even("lat")
    at_a, at_b = jnp.where(is_even, low, top), jnp.where(is_even, top, low)
    for r in range(HALF):
        a_ref[r * LEV : (r + 1) * LEV, :] = source_ref[at_a + r]
        b_ref[r * LEV : (r + 1) * LEV, :] = source_ref[at_b + r]


def push_rows(g_ref, weight_ref, wide):
    group = 4
    for first in range(0, ROWS + 2 * HALF, group):
        totals = [jnp.zeros((LEV, COLS), F32) for _ in range(group)]
        for j in range(max(0, first - 2 * HALF), min(ROWS, first + group)):
            g = g_ref[j]
            for n in range(group):
                distance = abs(first + n - HALF - j)
                if distance <= HALF:
                    totals[n] = totals[n] + weight_ref[distance, j : j + 1, :] * g
        for n in range(group):
            wide[first + n] = totals[n]


def push_out(g_ref, weight_ref, wide, mid_ref, a_ref, b_ref):
    push_rows(g_ref, weight_ref, wide)
    mid_ref[...] = wide[HALF : HALF + ROWS]
    copy_sides(wide, 0, HALF + ROWS, a_ref, b_ref)


def scatter_rhs_kernel(
    got_ref, local_ref, mid_ref, a_ref, b_ref, turned_ref, sigma_rows_ref, lat_weight_ref, *refs
):
    work, (sums, g, wide) = refs[:8], refs[8:]
    turned_ref[...] = got_ref[...].T
    scale = local_ref[CELLS:, :]
    factor = -0.5 / (scale * scale)
    norm = jnp.ones_like(factor)
    for d in range(1, HALF + 1):
        raw = jnp.exp(float(d * d) * factor)
        lat_weight_ref[d] = raw
        norm = norm + 2.0 * raw
    inverse = 1.0 / norm
    lat_weight_ref[0] = inverse
    for d in range(1, HALF + 1):
        lat_weight_ref[d] = lat_weight_ref[d] * inverse
    sums[...] = jnp.zeros_like(sums)
    accumulate(turned_ref, RHS, work, sums)
    for j in range(ROWS):
        sigma = row_of(local_ref, j)
        sigma_rows_ref[j] = sigma
        g[j] = sigma * two_rows(sums, 0, j)
    push_out(g, lat_weight_ref, wide, mid_ref, a_ref, b_ref)


OPERATOR = DIAG + EAST + NORTH
CUTS = (0, 16, 40, CAP)


def operator_kernel(begin, end, turned_ref, *refs):
    refs = list(refs)
    before_ref = refs.pop(0) if begin > 0 else None
    if end < CAP:
        sums, work = refs[0], refs[1:]
    else:
        outs, sums, work = refs[:5], refs[5], refs[6:]
    sums[...] = jnp.zeros_like(sums) if begin == 0 else before_ref[...]
    accumulate(turned_ref, OPERATOR, work, sums, begin, end)
    if end < CAP:
        return
    for j in range(ROWS):
        outs[0][j] = two_rows(sums, 0, j)
        outs[1][j] = two_rows(sums, 2, j)
        for n in range(3):
            outs[2 + n][j] = base_row(sums, 4 + n, j) if j < BASE_ROWS else jnp.zeros((LEV, COLS), F32)


def field_shape(rows=ROWS):
    return jax.ShapeDtypeStruct((rows, LEV, COLS), F32)


def scatter_scratch(count):
    return [
        pltpu.VMEM((ROWS_PAD, CHUNK * 128), BF16),
        pltpu.VMEM((count * 128, CHUNK * 128), BF16),
        pltpu.VMEM((ROWS_PAD, CHUNK * 128), F8),
        pltpu.VMEM((count * 128, CHUNK * 128), F8),
    ] * 2


def rim_shape():
    return jax.ShapeDtypeStruct((HALF * LEV, COLS), F32)


def sums_shape(count):
    return (count, ROWS_PAD, COLS)


def row_scratch():
    return [pltpu.VMEM((ROWS, LEV, COLS), F32), pltpu.VMEM((ROWS + 2 * HALF, LEV, COLS), F32)]


def scatter_cost(count, slots=CAP):
    return pl.CostEstimate(
        flops=4 * ROWS_PAD * OWNERS * slots * 128 * count, bytes_accessed=2 * 1024 * 1024, transcendentals=0
    )


def scatter_rhs(got, local):
    return pl.pallas_call(
        scatter_rhs_kernel,
        out_shape=[
            field_shape(),
            rim_shape(),
            rim_shape(),
            jax.ShapeDtypeStruct((FIELDS * CAP, OWNERS), F32),
            field_shape(),
            jax.ShapeDtypeStruct((HALF + 1, ROWS, COLS), F32),
        ],
        scratch_shapes=scatter_scratch(2) + [pltpu.VMEM(sums_shape(2), F32)] + row_scratch(),
        compiler_params=params(9),
        cost_estimate=scatter_cost(2),
        name="scatter_rhs",
    )(got, local)


def scatter_operator(turned, part, *before):
    begin, end = CUTS[part], CUTS[part + 1]
    count = len(OPERATOR)
    final = end == CAP
    running = jax.ShapeDtypeStruct(sums_shape(count), F32)
    return pl.pallas_call(
        functools.partial(operator_kernel, begin, end),
        out_shape=[field_shape()] * 5 if final else running,
        scratch_shapes=([pltpu.VMEM(sums_shape(count), F32)] if final else []) + scatter_scratch(count),
        compiler_params=params(18),
        cost_estimate=scatter_cost(count, end - begin),
        name="scatter_operator",
    )(turned, *before)


NEAR_TILE = tuple(range(0, 160, 16)) + (224, 240)
NEAR_SIDE = (0, 16) + tuple(range(96, 176, 16)) + (208, 224, 240)


def weights_kernel(
    lon_ref, a_ref, b_ref, high_ref, low_ref, inverse_ref,
    square, factors, columns, plain_high, plain_low, turned_high, turned_low,
):
    offset = ((iota((256, 256), 0) - iota((256, 256), 1) + 128) & 255) - 128
    square[...] = jnp.where(jnp.abs(offset) <= HALF, (offset * offset).astype(F32), 1e30)
    for ref in (plain_high, plain_low, turned_high, turned_low):
        ref[...] = jnp.zeros_like(ref)

    is_even = even("lon")
    east, west = jnp.where(is_even, a_ref[...], b_ref[...]), jnp.where(is_even, b_ref[...], a_ref[...])
    lane = iota((ROWS, COLS), 1)
    valid = jnp.logical_or(lane < HALO_COLS, lane >= COLS - HALO_COLS)
    beside = jnp.where(lane < HALO_COLS, east, jnp.where(valid, west, 1.0))
    for n, scale in enumerate((lon_ref[...], beside)):
        factor = -0.5 / (scale * scale)
        norm = jnp.ones_like(factor)
        for d in range(1, HALF + 1):
            norm = norm + 2.0 * jnp.exp(float(d * d) * factor)
        inverse = 1.0 / norm
        if n == 1:
            inverse = jnp.where(valid, inverse, 0.0)
        inverse_ref[:, n * COLS : (n + 1) * COLS] = inverse
        factors[n, :ROWS] = factor
        factors[n, ROWS:] = jnp.zeros((COLS - ROWS, COLS), F32)
        turned = factors[n].T
        for g in range(ROWS // 8):
            columns[g, n * 128 : (n + 1) * 128] = turned if g == 0 else pltpu.roll(turned, COLS - 8 * g, 1)

    def group(g, carry):
        for jj in range(8):
            j, n = 8 * g + jj, jj % 2
            factor = factors[0, pl.ds(j, 1), :]
            for r in range(0, 256, 16):
                at = slice(r, r + 16)
                column = jnp.broadcast_to(columns[g, at, jj : jj + 1], (16, 128))
                if r in NEAR_TILE:
                    high, low = split(jnp.exp(square[at, :128] * column))
                    plain_high[n, at, :128] = high.astype(BF16)
                    plain_low[n, at, :128] = low.astype(BF16)
                    high_ref[j, at, :128] = high.astype(BF16)
                    low_ref[j, at, :128] = low.astype(BF16)
                    high, low = split(jnp.exp(square[at, :128] * factor))
                    turned_high[n, at] = high.astype(BF16)
                    turned_low[n, at] = low.astype(BF16)
                else:
                    high_ref[j, at, :128] = jnp.zeros((16, 128), BF16)
                    low_ref[j, at, :128] = jnp.zeros((16, 128), BF16)
                if r in NEAR_SIDE:
                    high, low = split(jnp.exp(square[at, 128:] * column))
                    plain_high[n, at, 128:] = high.astype(BF16)
                    plain_low[n, at, 128:] = low.astype(BF16)
            gram = jnp.dot(plain_high[n], turned_high[n], preferred_element_type=F32)
            gram += jnp.dot(plain_low[n], turned_high[n], preferred_element_type=F32)
            gram += jnp.dot(plain_high[n], turned_low[n], preferred_element_type=F32)
            high, low = split(gram)
            high_ref[j, :, 128:] = high.astype(BF16)
            low_ref[j, :, 128:] = low.astype(BF16)
        return carry

    lax.fori_loop(0, ROWS // 8, group, 0)


def filter_weights(scale_lon, side_a, side_b):
    return pl.pallas_call(
        weights_kernel,
        out_shape=[jax.ShapeDtypeStruct((ROWS, 256, 256), BF16)] * 2 + [jax.ShapeDtypeStruct((ROWS, 256), F32)],
        scratch_shapes=[
            pltpu.VMEM((256, 256), F32),
            pltpu.VMEM((2, COLS, COLS), F32),
            pltpu.VMEM((ROWS // 8, 256, COLS), F32),
            pltpu.VMEM((2, 256, 256), BF16),
            pltpu.VMEM((2, 256, 256), BF16),
            pltpu.VMEM((2, 256, 128), BF16),
            pltpu.VMEM((2, 256, 128), BF16),
        ],
        compiler_params=params(9),
        cost_estimate=pl.CostEstimate(flops=2 * 10**9, bytes_accessed=8 * 1024 * 1024, transcendentals=0),
        name="filter_weights",
    )(scale_lon, side_a, side_b)


def lon_kernel(
    q_ref, ra_ref, rb_ref, high_ref, low_ref, inverse_ref, back_ref, mid_ref, a_ref, b_ref, norm_ref, wide, both
):
    lane = iota((LEV, COLS), 1)
    is_even = even("lon")
    wide[...] = jnp.zeros_like(wide)
    norm = jnp.zeros((LEV, COLS), F32)
    for j in range(ROWS):
        group, place_in = j // 3, j % 3
        ra, rb = ra_ref[group], rb_ref[group]
        east, west = jnp.where(is_even, ra, rb), jnp.where(is_even, rb, ra)
        west = pltpu.roll(west, (COLS - HALO_COLS - HALO_COLS * place_in) % COLS, 1)
        east = pltpu.roll(east, (-HALO_COLS * place_in) % COLS, 1)
        beside = jnp.where(lane < HALO_COLS, east, jnp.where(lane >= COLS - HALO_COLS, west, 0.0))
        wide[j % 4, :LEV, :COLS] = q_ref[j]
        wide[j % 4, :LEV, COLS:] = beside
        high, low = split(wide[j % 4] * inverse_ref[j : j + 1, :])
        both[j % 4, :32, :] = high.astype(BF16)
        both[j % 4, 32:, :] = low.astype(BF16)
        twice = jnp.dot(both[j % 4], high_ref[j], preferred_element_type=F32)
        more = jnp.dot(both[j % 4, :32, :], low_ref[j], preferred_element_type=F32)
        out = twice[:32] + twice[32:] + more
        back = out[:LEV, :COLS]
        back_ref[j] = back
        norm = norm + back * back
        mid_ref[j] = out[:LEV, COLS:] * inverse_ref[j : j + 1, :COLS]
    norm_ref[...] = norm
    copy_sides(mid_ref, 0, ROWS - HALF, a_ref, b_ref)


def lon_both(q, from_a, from_b, weights):
    return pl.pallas_call(
        lon_kernel,
        out_shape=[
            field_shape(),
            field_shape(),
            rim_shape(),
            rim_shape(),
            jax.ShapeDtypeStruct((LEV, COLS), F32),
        ],
        scratch_shapes=[pltpu.VMEM((4, 32, 256), F32), pltpu.VMEM((4, 64, 256), BF16)],
        compiler_params=params(9),
        name="lon_transpose_and_lon",
    )(q, from_a, from_b, *weights)


def fold_kernel(mid_ref, ra_ref, rb_ref, q_ref, a_ref, b_ref):
    is_even = even("lat")
    at_a = jnp.where(is_even, ROWS - HALF, 0)
    at_b = jnp.where(is_even, 0, ROWS - HALF)
    q_ref[...] = mid_ref[...]
    for r in range(HALF):
        q_ref[at_a + r] += ra_ref[r * LEV : (r + 1) * LEV, :]
    for r in range(HALF):
        q_ref[at_b + r] += rb_ref[r * LEV : (r + 1) * LEV, :]
    lane = iota((LEV, COLS), 1)
    is_even = even("lon")
    for group in range(ROWS // 3):
        west, east = 0.0, 0.0
        for n in range(3):
            value = q_ref[3 * group + n]
            here = jnp.logical_and(lane >= n * HALO_COLS, lane < (n + 1) * HALO_COLS)
            west = jnp.where(here, pltpu.roll(value, n * HALO_COLS, 1), west)
            east = jnp.where(here, pltpu.roll(value, (n + 1) * HALO_COLS, 1), east)
        a_ref[group] = jnp.where(is_even, east, west)
        b_ref[group] = jnp.where(is_even, west, east)


def fold(mid, from_a, from_b):
    pack = field_shape(ROWS // 3)
    return pl.pallas_call(
        fold_kernel,
        out_shape=[field_shape(), pack, pack],
        compiler_params=params(6),
        name="fold_rims",
    )(mid, from_a, from_b)


def lat_rows(mid_ref, ra_ref, rb_ref, wide, weight_ref, sigma_ref, image_ref):
    is_even = even("lat")
    at_a = jnp.where(is_even, HALF + ROWS, 0)
    at_b = jnp.where(is_even, 0, HALF + ROWS)
    wide[HALF : HALF + ROWS] = mid_ref[...]
    for r in range(HALF):
        wide[at_a + r] = ra_ref[r * LEV : (r + 1) * LEV, :]
        wide[at_b + r] = rb_ref[r * LEV : (r + 1) * LEV, :]
    group = 4
    for first in range(0, ROWS, group):
        totals = [jnp.zeros((LEV, COLS), F32) for _ in range(group)]
        for r in range(first, first + group + 2 * HALF):
            x = wide[r]
            for n in range(group):
                distance = abs(first + n + HALF - r)
                if distance <= HALF:
                    m = first + n
                    totals[n] = totals[n] + weight_ref[distance, m : m + 1, :] * x
        for n in range(group):
            image_ref[first + n] = sigma_ref[first + n] * totals[n]


def stencil(m, x_ref, diag_ref, east_ref, north_ref, north_east_ref, north_west_ref):
    x = x_ref[m]
    right = lambda value: pltpu.roll(value, COLS - 1, 1)
    out = diag_ref[m] * x + east_ref[m] * right(x)
    moved = east_ref[m] * x
    if m + 1 < ROWS:
        above = x_ref[m + 1]
        out = out + north_ref[m] * above + north_east_ref[m] * right(above)
        moved = moved + north_west_ref[m] * above
    if m > 0:
        below = x_ref[m - 1]
        out = out + north_ref[m - 1] * below + north_west_ref[m - 1] * right(below)
        moved = moved + north_east_ref[m - 1] * below
    return x, out + pltpu.roll(moved, 1, 1)


def observe_kernel(ra_ref, rb_ref, e_ref, weight_ref, sigma_ref, *refs):
    coefficients, (image_ref, mid_ref, a_ref, b_ref, norm_ref, g, wide) = refs[:5], refs[5:]
    lat_rows(e_ref, ra_ref, rb_ref, wide, weight_ref, sigma_ref, image_ref)
    norm = jnp.zeros((LEV, COLS), F32)
    for m in range(ROWS):
        x, out = stencil(m, image_ref, *coefficients)
        norm = norm + x * out
        g[m] = sigma_ref[m] * out
    norm_ref[...] = norm
    push_out(g, weight_ref, wide, mid_ref, a_ref, b_ref)


def observe(from_a, from_b, mid, lat_weight, sigma, coefficients):
    return pl.pallas_call(
        observe_kernel,
        out_shape=[
            field_shape(),
            field_shape(),
            rim_shape(),
            rim_shape(),
            jax.ShapeDtypeStruct((LEV, COLS), F32),
        ],
        scratch_shapes=row_scratch(),
        compiler_params=params(9),
        name="lat_and_observe",
    )(from_a, from_b, mid, lat_weight, sigma, *coefficients)


def last_kernel(ra_ref, rb_ref, e_ref, weight_ref, sigma_ref, *refs):
    coefficients, norm_refs, (image_ref, sums_ref, wide) = refs[:5], refs[5:8], refs[8:]
    lat_rows(e_ref, ra_ref, rb_ref, wide, weight_ref, sigma_ref, image_ref)
    norm = jnp.zeros((LEV, COLS), F32)
    for m in range(ROWS):
        x, out = stencil(m, image_ref, *coefficients)
        norm = norm + x * out
    lane = iota((1, 128), 1)
    row = jnp.zeros((1, 128), F32)
    for n, value in enumerate([ref[...] for ref in norm_refs] + [norm]):
        total = jnp.sum(jnp.sum(value, axis=0, keepdims=True), axis=1, keepdims=True)
        row = jnp.where(lane == n, total, row)
    sums_ref[...] = jnp.broadcast_to(row, (OWNERS, 128))


def last(from_a, from_b, mid, lat_weight, sigma, coefficients, norms):
    return pl.pallas_call(
        last_kernel,
        out_shape=[field_shape(), jax.ShapeDtypeStruct((OWNERS, 128), F32)],
        scratch_shapes=row_scratch()[1:],
        compiler_params=params(9),
        name="lat_and_moments",
    )(from_a, from_b, mid, lat_weight, sigma, *coefficients, *norms)


def exchange(axis, periodic, side_a, side_b):
    count = lax.axis_size(axis)

    def swaps(first):
        pairs = []
        for i in range(first, count, 2):
            if i + 1 < count or periodic:
                pairs += [(i, (i + 1) % count), ((i + 1) % count, i)]
        return pairs

    from_b = lax.ppermute(side_b, axis, swaps(1))
    return lax.ppermute(side_a, axis, swaps(0)), from_b


def combine_kernel(sums_ref, start_ref, start_image_ref, next_ref, next_image_ref, control_ref, increment_ref):
    row = jnp.sum(sums_ref[...], axis=0, keepdims=True)
    lane = iota((1, 128), 1)
    pick = lambda n: jnp.sum(jnp.where(lane == n, row, 0.0), axis=1, keepdims=True)
    m0 = pick(0)
    m1, m2, m3 = pick(1) / m0, pick(2) / m0, pick(3) / m0
    lift = 1.0 / (DAMP * DAMP)
    unit = 1.0 / lift
    step0 = unit / (unit + m1)
    keep = m1 / (unit + m1)
    ratio = jnp.maximum(m2 - m1 * m1, 0.0) / ((unit + m1) * (unit + m1))
    lead = keep + ratio
    tail = 1.0 / (unit + m1)
    second = lift * (lead * lead * m1 - 2.0 * lead * tail * m2 + tail * tail * m3)
    step1 = ratio / (ratio + ratio * ratio + second)
    alpha = step0 + step1 * lead
    gamma = -step1 * tail
    for j in range(ROWS):
        at = pl.ds(j, LEV, stride=ROWS)
        control_ref[at, :] = alpha * start_ref[j] + gamma * next_ref[j]
        increment_ref[at, :] = alpha * start_image_ref[j] + gamma * next_image_ref[j]


def combine(sums, start, start_image, following, following_image):
    return pl.pallas_call(
        combine_kernel,
        out_shape=[jax.ShapeDtypeStruct((CELLS, COLS), F32)] * 2,
        compiler_params=params(9),
        name="combine",
    )(sums, start, start_image, following, following_image)


def body(
    background_sigma,
    scale_lon,
    scale_lat,
    obs_owner,
    obs_count,
    obs_cell,
    obs_level,
    obs_weight,
    obs_value,
    obs_precision,
):
    everyone = ("lon", "lat")
    send = place(obs_owner, obs_count, obs_cell, obs_level, obs_weight, obs_value, obs_precision)
    send, scale_lon = lax.optimization_barrier((send, scale_lon))
    got = lax.all_to_all(send, everyone, 0, 0, tiled=True).reshape(OWNERS, FIELDS * CAP)
    scale_a, scale_b = exchange("lon", True, scale_lon, scale_lon)
    local = jnp.concatenate([background_sigma.reshape(CELLS, COLS), scale_lat], axis=0)
    mid, side_a, side_b, turned, sigma, lat_weight = scatter_rhs(got, local)
    turned, scale_lon, scale_a, scale_b = lax.optimization_barrier((turned, scale_lon, scale_a, scale_b))
    lon_weight = filter_weights(scale_lon, scale_a, scale_b)

    from_a, from_b = exchange("lat", False, side_a, side_b)
    sums = scatter_operator(turned, 0)
    q, side_a, side_b = fold(mid, from_a, from_b)
    from_a, from_b = exchange("lon", True, side_a, side_b)
    sums = scatter_operator(turned, 1, sums)
    start, mid, side_a, side_b, norm0 = lon_both(q, from_a, from_b, lon_weight)
    from_a, from_b = exchange("lat", False, side_a, side_b)
    coefficients = scatter_operator(turned, 2, sums)
    image0, mid, side_a, side_b, norm1 = observe(from_a, from_b, mid, lat_weight, sigma, coefficients)

    from_a, from_b = exchange("lat", False, side_a, side_b)
    q, side_a, side_b = fold(mid, from_a, from_b)
    from_a, from_b = exchange("lon", True, side_a, side_b)
    following, mid, side_a, side_b, norm2 = lon_both(q, from_a, from_b, lon_weight)
    from_a, from_b = exchange("lat", False, side_a, side_b)
    image1, sums = last(from_a, from_b, mid, lat_weight, sigma, coefficients, (norm0, norm1, norm2))
    sums = lax.all_to_all(sums, everyone, 0, 0, tiled=True)
    control, increment = combine(sums, start, image0, following, image1)
    shape = background_sigma.shape
    return control.reshape(shape), increment.reshape(shape)


def solution(mesh):
    return jax.shard_map(
        body,
        mesh=mesh,
        in_specs=(
            P(None, "lat", "lon"),
            P("lat", "lon"),
            P("lat", "lon"),
            P(("lon", "lat")),
            P(("lon", "lat")),
            P(("lon", "lat")),
            P(("lon", "lat")),
            P(None, ("lon", "lat")),
            P(("lon", "lat")),
            P(("lon", "lat")),
        ),
        out_specs=(P(None, "lat", "lon"), P(None, "lat", "lon")),
        check_vma=False,
    )
```
